256 devices in a mesh: dp: 32 (over z_hi, y, core), ctr: 8 (over z_lo, x).
Axes of the slice: x: 4, y: 4, z: 8 (z_hi: 4, z_lo: 2; z = z_hi * 2 + z_lo), core: 2. Of those that a mesh axis runs over, the one named last changes fastest.
Arguments:
- points: bfloat16 [65536, 128], P(('dp', 'ctr')), may hold values from -6 to 6
- adjoint_rows: bfloat16 [65536, 32], P(('dp', 'ctr')), may hold values from -8 to 8
- centers: bfloat16 [32768, 128], P(('dp', 'ctr')), may hold values from -6 to 6
- solution_rows: bfloat16 [32768, 32], P(('dp', 'ctr')), may hold values from -8 to 8
- center_left: bfloat16 [32768, 32], P(('dp', 'ctr')), may hold values from -8 to 8
- center_right: bfloat16 [32768, 32], P(('dp', 'ctr')), may hold values from -8 to 8
- lengthscale: float32 [128], replicated, may hold values from 6 to 24
Outputs:
- grad_centers: float32 [32768, 128], P(('dp', 'ctr'))
- grad_scale: float32 [128], replicated
The draws below stay inside these ranges and needn't reach their ends.
All inputs are finite; a program needn't handle non-finite values.
Results may differ from the reference program's by a relative error of at most 0.0047.
Values may be sent and summed in bfloat16 or wider, within the bound.
No kernel may reach another device: no remote copies, remote signals or barrier semaphores. Data moves between devices by JAX's collectives and lax.ppermute only.
A program may use at most 64 MiB of HBM per device.

```python
import math
import jax
import jax.numpy as jnp
from jax import lax

D = 128
R = 32
ROWS = 65536
CENTERS = 32768


def row_scales(key, rows, base):
    ramp = 3.0 ** (jnp.arange(rows, dtype=jnp.float32) / max(rows - 1, 1))
    rough = jnp.exp(jax.random.uniform(key, (rows, 1), jnp.float32, -1.15, 1.15))
    return base * ramp[:, None] * rough


def entries_normal(key, rows, cols):
    return jax.random.truncated_normal(key, -4.0, 4.0, (rows, cols), jnp.float32)


def draw_adjoint_rows(key, part):
    key = jax.random.fold_in(key, 11)
    first, second = jax.random.split(key)
    values = entries_normal(first, ROWS, R)
    return (values * row_scales(second, ROWS, 0.2)).astype(jnp.bfloat16)


def draw_solution_rows(key, part):
    key = jax.random.fold_in(key, 23)
    first, second = jax.random.split(key)
    values = entries_normal(first, CENTERS, R)
    return (values * row_scales(second, CENTERS, 0.2)).astype(jnp.bfloat16)


def draw_center_left(key, part):
    key = jax.random.fold_in(key, 37)
    first, second = jax.random.split(key)
    values = entries_normal(first, CENTERS, R)
    return (values * row_scales(second, CENTERS, 0.2)).astype(jnp.bfloat16)


def draw_center_right(key, part):
    key = jax.random.fold_in(key, 41)
    first, second = jax.random.split(key)
    values = entries_normal(first, CENTERS, R)
    return (values * row_scales(second, CENTERS, 0.2)).astype(jnp.bfloat16)


def levels(stream_key, extent, cuts, smallest, largest):
    def one(axis_at, parts):
        heights = jax.random.uniform(jax.random.fold_in(jax.random.fold_in(stream_key, 6), axis_at), (parts,), jnp.float32, smallest / len(cuts), largest / len(cuts))
        return jnp.repeat(jnp.exp(heights), extent[axis_at] // parts).reshape((-1,) + (1,) * (len(extent) - axis_at - 1))

    factor_of = one(*cuts[0])
    for cut in cuts[1:]:
        factor_of = factor_of * one(*cut)
    return factor_of


def normal_values(own_key, shape, spread, most, cuts=(), kind=jnp.bfloat16):
    array = jax.random.normal(own_key, shape, jnp.float32) * spread
    if len(cuts) > 0:
        array = levels(own_key, shape, cuts, -0.22, 0.18) * array
    return jnp.clip(array, min=-most, max=most).astype(kind)


def setup_inputs(seed: int = 0) -> dict:
    seeds = jax.random.split(jax.random.key(seed), 8)
    points = normal_values(seeds[0], (ROWS, D), 1.0, 6.0, ((0, 256),))
    adjoint_rows = draw_adjoint_rows(jax.random.fold_in(seeds[7], 71), 0)
    centers = normal_values(seeds[2], (CENTERS, D), 1.0, 6.0, ((0, 256),))
    solution_rows = draw_solution_rows(jax.random.fold_in(seeds[7], 71), 0)
    center_left = draw_center_left(jax.random.fold_in(seeds[7], 71), 0)
    center_right = draw_center_right(jax.random.fold_in(seeds[7], 71), 0)
    lengthscale = jnp.clip(jnp.exp(jax.random.uniform(seeds[6], (D,), jnp.float32, math.log(6.0), math.log(24.0))), 6.0, 24.0)
    return dict(points=points, adjoint_rows=adjoint_rows, centers=centers, solution_rows=solution_rows, center_left=center_left, center_right=center_right, lengthscale=lengthscale)


def gauss(left, left_sq, right, right_sq):
    cross = jnp.dot(left, right.T, preferred_element_type=jnp.float32)
    return jnp.exp(-0.5 * (left_sq[:, None] + right_sq[None, :] - 2.0 * cross))


def reference(points, adjoint_rows, centers, solution_rows, center_left, center_right, lengthscale):
    scaled_x = (points.astype(jnp.float32) / lengthscale).astype(jnp.bfloat16)
    scaled_c = (centers.astype(jnp.float32) / lengthscale).astype(jnp.bfloat16)
    xfull = scaled_x.astype(jnp.float32)
    cfull = scaled_c.astype(jnp.float32)
    x_sq = jnp.sum(xfull * xfull, 1)
    c_sq = jnp.sum(cfull * cfull, 1)
    row_blk = math.gcd(ROWS, 2048)
    row_cnt = ROWS // row_blk

    def data_step(carry, item):
        g_acc, col_acc, ell_acc = carry
        xblock, vblock, xsq_block = item
        kern = gauss(xblock, xsq_block, scaled_c, c_sq)
        weight = kern * jnp.dot(vblock, solution_rows.T, preferred_element_type=jnp.float32)
        rounded = weight.astype(jnp.bfloat16)
        g_acc = g_acc + jnp.dot(rounded.T, xblock, preferred_element_type=jnp.float32)
        col_acc = col_acc + jnp.sum(weight, 0)
        xblock_f = xblock.astype(jnp.float32)
        ell_acc = ell_acc + jnp.sum(jnp.sum(weight, 1)[:, None] * xblock_f * xblock_f, 0)
        return (g_acc, col_acc, ell_acc), None

    init = (jnp.zeros((CENTERS, D), jnp.float32), jnp.zeros((CENTERS,), jnp.float32), jnp.zeros((D,), jnp.float32))
    (data_g, data_col, ell_acc), unused = lax.scan(
        data_step, init,
        (scaled_x.reshape(row_cnt, row_blk, D), adjoint_rows.reshape(row_cnt, row_blk, R), x_sq.reshape(row_cnt, row_blk)))

    ctr_blk = math.gcd(CENTERS, 2048)
    ctr_cnt = CENTERS // ctr_blk

    def pair_step(carry, item):
        col_g, col_q = carry
        cblock, ablock, csq_block = item
        kern = gauss(cblock, csq_block, scaled_c, c_sq)
        weight = kern * jnp.dot(ablock, center_right.T, preferred_element_type=jnp.float32)
        rounded = weight.astype(jnp.bfloat16)
        row_g = jnp.dot(rounded, scaled_c, preferred_element_type=jnp.float32)
        row_q = jnp.sum(weight, 1)
        col_g = col_g + jnp.dot(rounded.T, cblock, preferred_element_type=jnp.float32)
        col_q = col_q + jnp.sum(weight, 0)
        return (col_g, col_q), (row_g, row_q)

    init2 = (jnp.zeros((CENTERS, D), jnp.float32), jnp.zeros((CENTERS,), jnp.float32))
    (col_g, col_q), (row_g, row_q) = lax.scan(
        pair_step, init2,
        (scaled_c.reshape(ctr_cnt, ctr_blk, D), center_left.reshape(ctr_cnt, ctr_blk, R), c_sq.reshape(ctr_cnt, ctr_blk)))
    row_g = row_g.reshape(CENTERS, D)
    row_q = row_q.reshape(CENTERS)
    total_q = data_col + row_q + col_q
    grad_centers = ((data_g + row_g + col_g) - total_q[:, None] * cfull) / lengthscale
    scale_sum = ell_acc + jnp.sum(total_q[:, None] * cfull * cfull, 0) - 2.0 * jnp.sum(cfull * (data_g + row_g), 0)
    return grad_centers, scale_sum / lengthscale
```

```python
import functools

import jax
import jax.numpy as jnp
from jax import lax
from jax.experimental import pallas as pl
from jax.experimental.pallas import tpu as pltpu
from jax.sharding import Mesh, PartitionSpec as P

BF = jnp.bfloat16
F32 = jnp.float32
AXES = ("zh", "y", "core", "zl", "x")
SIZES = (4, 4, 2, 2, 4)
CENTER_AXES = ("zl", "x")
PARTNER_AXES = ("zh", "y")
D = 128
R = 32
PTS = 256
CTR = 128
CROWS = CTR + 3 * R
PROWS = PTS + CTR + 4 * R
TROWS = CTR + 8


def dot_nt(a, b):
    return lax.dot_general(a, b, (((1,), (1,)), ((), ())), preferred_element_type=F32)


def dot_nn(a, b):
    return lax.dot_general(a, b, (((1,), (0,)), ((), ())), preferred_element_type=F32)


def prep_kernel(x_ref, v_ref, c_ref, s_ref, l_ref, r_ref, ls_ref, pp_ref, cp_ref, pbuf, cbuf, sem, *, np_, nc):
    ls = ls_ref[...]
    pbuf[0:PTS, :] = (x_ref[...].astype(F32) / ls).astype(BF)
    c = (c_ref[...].astype(F32) / ls).astype(BF)
    pbuf[PTS : PTS + CTR, :] = c
    cbuf[0:CTR, :] = c
    base = PTS + CTR
    vt = v_ref[...].astype(F32).T.astype(BF)
    pbuf[base : base + R, :] = vt[:, 0:CTR]
    pbuf[base + R : base + 2 * R, :] = vt[:, CTR : 2 * CTR]
    lt = l_ref[...].astype(F32).T.astype(BF)
    rt = r_ref[...].astype(F32).T.astype(BF)
    pbuf[base + 2 * R : base + 3 * R, :] = rt
    pbuf[base + 3 * R : base + 4 * R, :] = lt
    cbuf[CTR : CTR + R, :] = s_ref[...].astype(F32).T.astype(BF)
    cbuf[CTR + R : CTR + 2 * R, :] = lt
    cbuf[CTR + 2 * R : CTR + 3 * R, :] = rt
    copies = [pltpu.make_async_copy(cbuf, cp_ref.at[i], sem.at[i]) for i in range(nc)]
    copies += [pltpu.make_async_copy(pbuf, pp_ref.at[i], sem.at[nc + i]) for i in range(np_)]
    for cp in copies:
        cp.start()
    for cp in copies:
        cp.wait()


def tail_columns(f, swap):
    n = f.shape[0]
    ff = f.astype(F32)
    h = -0.5 * jnp.sum(ff * ff, axis=1, keepdims=True)
    a = h.astype(BF).astype(F32)
    rest = h - a
    b = rest.astype(BF).astype(F32)
    c = rest - b
    lane = lax.broadcasted_iota(jnp.int32, (n, 128), 1)
    o, one = (3, 0) if swap else (0, 3)
    t = jnp.where((lane >= one) & (lane < one + 3), 1.0, 0.0)
    t = jnp.where(lane == o + 2, c, t)
    t = jnp.where(lane == o + 1, b, t)
    t = jnp.where(lane == o, a, t)
    return t.astype(BF)


def main_kernel(own_ref, oth_ref, pp_ref, ls_ref, t_ref, ca, us, ul, gd, gp, qa, ell):
    nc = own_ref.shape[0]
    npeer = pp_ref.shape[0]
    m = 2 * nc * CTR
    lane = lax.broadcasted_iota(jnp.int32, (CTR, 128), 1)
    for j in range(2 * nc):
        ref, k = (own_ref, j) if j < nc else (oth_ref, j - nc)
        rows = slice(j * CTR, (j + 1) * CTR)
        c = ref[k, 0:CTR, :]
        ca[rows, 0:D] = c
        ca[rows, D : 2 * D] = tail_columns(c, False)
        ut = jnp.concatenate([ref[k, CTR:CROWS, :], jnp.zeros((R, 128), BF)], 0)
        u = ut.astype(F32).T
        us[rows, :] = jnp.where(lane < R, u, 0.0).astype(BF)
        ul[rows, :] = jnp.where((lane >= R) & (lane < 3 * R), u, 0.0).astype(BF)
    gd[...] = jnp.zeros_like(gd)
    gp[...] = jnp.zeros_like(gp)
    qa[...] = jnp.zeros_like(qa)
    ell[...] = jnp.zeros_like(ell)

    def sweep(x, vt, u_ref, g_ref):
        n = x.shape[0]
        xt = jnp.concatenate([x, tail_columns(x, True)], 1)
        kern = jnp.exp(dot_nt(ca[...], xt))
        w = kern * dot_nn(u_ref[...], vt)
        g_ref[...] += dot_nn(w.astype(BF), x)
        s = w[:, 0:128]
        for k in range(1, n // 128):
            s = s + w[:, k * 128 : (k + 1) * 128]
        qa[...] += s
        return w

    def step(a, carry):
        ia, ib = 2 * a, 2 * a + 1
        base = PTS + CTR
        x = jnp.concatenate([pp_ref[ia, 0:PTS, :], pp_ref[ib, 0:PTS, :]], 0)
        vt = jnp.concatenate(
            [pp_ref[i, base + k * R : base + (k + 1) * R, :] for i in (ia, ib) for k in (0, 1)], 1
        )
        vt = jnp.concatenate([vt, jnp.zeros((3 * R, 2 * PTS), BF)], 0)
        w = sweep(x, vt, us, gd)
        rowsum = jnp.sum(w.reshape(m // 8, 8, 2 * PTS), axis=0)
        r1 = rowsum.astype(BF)
        rest = rowsum - r1.astype(F32)
        r2 = rest.astype(BF)
        r3 = (rest - r2.astype(F32)).astype(BF)
        xf = x.astype(F32)
        xsq = xf * xf
        xh = xsq.astype(BF)
        xl = (xsq - xh.astype(F32)).astype(BF)
        ell[...] += dot_nn(
            jnp.concatenate([r1, r2, r3, jnp.zeros_like(r1)], 0), jnp.concatenate([xh, xl], 1)
        )
        c = jnp.concatenate([pp_ref[ia, PTS:base, :], pp_ref[ib, PTS:base, :]], 0)
        z = jnp.zeros((R, 2 * CTR), BF)
        vc = jnp.concatenate([pp_ref[ia, base + 2 * R : PROWS, :], pp_ref[ib, base + 2 * R : PROWS, :]], 1)
        sweep(c, jnp.concatenate([z, vc, z], 0), ul, gp)
        return carry

    lax.fori_loop(0, npeer // 2, step, 0)

    e = ell[...]
    e = e[:, 0:128] + e[:, 128:256]
    scale = e[0:8] + e[8:16] + e[16:24]
    ls = ls_ref[...]
    for j in range(2 * nc):
        rows = slice(j * CTR, (j + 1) * CTR)
        c = ca[rows, 0:D].astype(F32)
        q = jnp.sum(qa[rows, :], axis=1, keepdims=True)
        g1 = gd[rows, :]
        g = g1 + gp[rows, :]
        qc = q * c
        t_ref[j // nc, j % nc, 0:CTR, :] = (g - qc) / ls
        part = c * (qc - (g + g1))
        scale = scale + jnp.sum(part.reshape(CTR // 8, 8, D), axis=0)
    for j in range(2 * nc):
        t_ref[j // nc, j % nc, CTR:TROWS, :] = scale


def local(points, adjoint_rows, centers, solution_rows, center_left, center_right, lengthscale):
    size = dict(zip(AXES, SIZES))
    nc = size["zl"] * size["x"]
    npeer = size["zh"] * size["y"]
    ls = lengthscale.reshape(1, D)
    vm = pl.BlockSpec(memory_space=pltpu.VMEM)
    hbm = pl.BlockSpec(memory_space=pl.ANY)
    pp, cp = pl.pallas_call(
        functools.partial(prep_kernel, np_=npeer, nc=nc),
        out_shape=[
            jax.ShapeDtypeStruct((npeer, PROWS, D), BF),
            jax.ShapeDtypeStruct((nc, CROWS, D), BF),
        ],
        in_specs=[vm] * 7,
        out_specs=[hbm, hbm],
        scratch_shapes=[
            pltpu.VMEM((PROWS, D), BF),
            pltpu.VMEM((CROWS, D), BF),
            pltpu.SemaphoreType.DMA((npeer + nc,)),
        ],
        name="prep",
    )(points, adjoint_rows, centers, solution_rows, center_left, center_right, ls)
    own = lax.all_to_all(cp, CENTER_AXES, 0, 0, tiled=True)
    oth = lax.ppermute(own, "core", [(0, 1), (1, 0)])
    partners = lax.all_to_all(pp, PARTNER_AXES, 0, 0, tiled=True)
    m = 2 * nc * CTR
    terms = pl.pallas_call(
        main_kernel,
        out_shape=jax.ShapeDtypeStruct((2, nc, TROWS, D), F32),
        in_specs=[vm] * 4,
        out_specs=vm,
        scratch_shapes=[
            pltpu.VMEM((m, 2 * D), BF),
            pltpu.VMEM((m, D), BF),
            pltpu.VMEM((m, D), BF),
            pltpu.VMEM((m, D), F32),
            pltpu.VMEM((m, D), F32),
            pltpu.VMEM((m, D), F32),
            pltpu.VMEM((32, 2 * D), F32),
        ],
        compiler_params=pltpu.CompilerParams(vmem_limit_bytes=48 * 2**20),
        name="pairs",
    )(own, oth, partners, ls)
    both = terms[0] + lax.ppermute(terms[1], "core", [(0, 1), (1, 0)])
    parts = lax.all_to_all(both, CENTER_AXES, 0, 0, tiled=True)
    total = jnp.sum(parts, 0)
    grad_centers = total[0:CTR]
    tiny = jnp.broadcast_to(total[CTR:TROWS][None], (npeer, 8, D))
    scale = jnp.sum(lax.all_to_all(tiny, PARTNER_AXES, 0, 0, tiled=True), (0, 1))
    return grad_centers, scale / lengthscale


def solution(mesh):
    grid = Mesh(mesh.devices.reshape(SIZES), AXES)
    rows = P(AXES, None)
    return jax.shard_map(
        local,
        mesh=grid,
        in_specs=(rows,) * 6 + (P(),),
        out_specs=(rows, P()),
        check_vma=False,
    )
```

```python
import functools

import jax
import jax.numpy as jnp
from jax import lax
from jax.experimental import pallas as pl
from jax.experimental.pallas import tpu as pltpu
from jax.sharding import Mesh, PartitionSpec as P

BF = jnp.bfloat16
F32 = jnp.float32
AXES = ("zh", "y", "core", "zl", "x")
SIZES = (4, 4, 2, 2, 4)
CENTER_AXES = ("zh", "zl")
BLOCK_AXES = ("zh", "zl", "core")
PLANE_AXES = ("y", "core", "x")
SCALE_AXES = ("y", "x", "core")
D = 128
R = 32
PTS = 256
CTR = 128
CROWS = CTR + 3 * R
BASE = PTS + CTR
PROWS = BASE + 4 * R
TAIL = 16
NZ = 8
NB = 2 * NZ
NSIDE = 4
M = NB * CTR
VM = pl.BlockSpec(memory_space=pltpu.VMEM)
SM = pl.BlockSpec(memory_space=pltpu.SMEM)
PARAMS = pltpu.CompilerParams(vmem_limit_bytes=44 * 2**20)


def dot_nn(a, b):
    return lax.dot_general(a, b, (((1,), (0,)), ((), ())), preferred_element_type=F32)


def fold(v):
    return jnp.sum(v.reshape(v.shape[0] // 8, 8, v.shape[1]), axis=0)


def prep_kernel(x_ref, v_ref, c_ref, s_ref, l_ref, r_ref, ls_ref, pp_ref, cb_ref):
    ls = ls_ref[...]
    x = (x_ref[...].astype(F32) / ls).astype(BF)
    c = (c_ref[...].astype(F32) / ls).astype(BF)
    lt, rt = l_ref[...], r_ref[...]
    pp_ref[...] = jnp.concatenate([x, c, v_ref[:, 0:CTR], v_ref[:, CTR:PTS], rt, lt], 0)
    cb_ref[...] = jnp.concatenate([c, s_ref[...], lt, rt], 0)


def set_centers(cen_ref, ca, hc, us, ul):
    lane = lax.broadcasted_iota(jnp.int32, (CTR, 128), 1)
    for j in range(NB):
        rows = slice(j * CTR, (j + 1) * CTR)
        c = cen_ref[j, 0:CTR, :]
        cf = c.astype(F32)
        ca[rows, :] = c
        hc[rows, :] = jnp.broadcast_to(0.5 * jnp.sum(cf * cf, axis=1, keepdims=True), (CTR, 128))
        ut = jnp.concatenate([cen_ref[j, CTR:CROWS, :], jnp.zeros((R, 128), BF)], 0)
        u = ut.astype(F32).T
        us[rows, :] = jnp.where(lane < R, u, 0.0).astype(BF)
        ul[rows, :] = jnp.where((lane >= R) & (lane < 3 * R), u, 0.0).astype(BF)


def turn(rows, xt, hx, slot, at):
    t = rows.astype(F32).T
    cols = slice(at * 128, (at + 1) * 128)
    xt[slot, :, cols] = t.astype(BF)
    hx[slot, :, cols] = jnp.broadcast_to(0.5 * jnp.sum(t * t, axis=0, keepdims=True), (8, 128))


def sweep(x, xt, hx, vt, ca, hc, u_ref, g, qa):
    n = x.shape[0]
    cross = dot_nn(ca[...], xt)
    prod = dot_nn(u_ref[...], vt)
    h = hc[...]
    parts = []
    for k in range(n // 128):
        cols = slice(k * 128, (k + 1) * 128)
        parts.append(jnp.exp((cross[:, cols] - h) - hx[:, cols]) * prod[:, cols])
    w = jnp.concatenate(parts, 1)
    g[...] += dot_nn(w.astype(BF), x)
    s = parts[0]
    for p in parts[1:]:
        s = s + p
    qa[...] += s
    return w


def add_pairs(blocks, count, ca, hc, us, ul, g, qa, ell, xt, hx, ct, hy):
    g[...] = jnp.zeros_like(g)
    qa[...] = jnp.zeros_like(qa)
    ell[...] = jnp.zeros_like(ell)
    steps = count // NSIDE

    def turn_points(a, slot):
        for k in range(NSIDE):
            turn(blocks[NSIDE * a + k, 0:128, :], xt, hx, slot, 2 * k)
            turn(blocks[NSIDE * a + k, 128:PTS, :], xt, hx, slot, 2 * k + 1)

    def turn_centers(a, slot):
        for k in range(NSIDE):
            turn(blocks[NSIDE * a + k, PTS:BASE, :], ct, hy, slot, k)

    def points_step(a, carry):
        ids = [NSIDE * a + k for k in range(NSIDE)]
        slot = lax.rem(a, 2)
        x = jnp.concatenate([blocks[i, 0:PTS, :] for i in ids], 0)
        vt = jnp.concatenate(
            [blocks[i, BASE + k * R : BASE + (k + 1) * R, :] for i in ids for k in (0, 1)], 1
        )
        vt = jnp.concatenate([vt, jnp.zeros((3 * R, NSIDE * PTS), BF)], 0)
        w = sweep(x, xt[slot], hx[slot, 0:1, :], vt, ca, hc, us, g, qa)
        if steps > 1:
            turn_points(lax.min(a + 1, steps - 1), 1 - slot)
        rowsum = fold(w)
        r1 = rowsum.astype(BF)
        rest = rowsum - r1.astype(F32)
        r2 = rest.astype(BF)
        r3 = (rest - r2.astype(F32)).astype(BF)
        xf = x.astype(F32)
        xsq = xf * xf
        xh = xsq.astype(BF)
        xl = (xsq - xh.astype(F32)).astype(BF)
        ell[...] += dot_nn(
            jnp.concatenate([r1, r2, r3, jnp.zeros_like(r1)], 0), jnp.concatenate([xh, xl], 1)
        )
        return carry

    def centers_step(a, carry):
        ids = [NSIDE * a + k for k in range(NSIDE)]
        slot = lax.rem(a, 2)
        c = jnp.concatenate([blocks[i, PTS:BASE, :] for i in ids], 0)
        z = jnp.zeros((R, NSIDE * CTR), BF)
        vc = jnp.concatenate([blocks[i, BASE + 2 * R : PROWS, :] for i in ids], 1)
        sweep(c, ct[slot], hy[slot, 0:1, :], jnp.concatenate([z, vc, z], 0), ca, hc, ul, g, qa)
        if steps > 1:
            turn_centers(lax.min(a + 1, steps - 1), 1 - slot)
        return carry

    turn_points(0, 0)
    lax.fori_loop(0, steps, points_step, 0)
    e = ell[...]
    e = e[:, 0:128] + e[:, 128:256]
    scale = e[0:8] + e[8:16] + e[16:24]
    for j in range(NB):
        rows = slice(j * CTR, (j + 1) * CTR)
        scale = scale - fold(ca[rows, :].astype(F32) * g[rows, :])
    turn_centers(0, 0)
    lax.fori_loop(0, steps, centers_step, 0)
    return scale


def block_terms(j, ca, g, qa):
    rows = slice(j * CTR, (j + 1) * CTR)
    c = ca[rows, :].astype(F32)
    q = jnp.sum(qa[rows, :], axis=1, keepdims=True)
    t = g[rows, :] - q * c
    return t, fold(c * t)


def first_kernel(cen_ref, a_ref, b_ref, c_ref, d_ref, ca, hc, us, ul, t_ref, s_ref, g, qa, ell, xt, hx, ct, hy, blocks):
    set_centers(cen_ref, ca, hc, us, ul)
    for k, ref in enumerate((a_ref, b_ref, c_ref, d_ref)):
        blocks[k] = ref[...]
    scale = add_pairs(blocks, NSIDE, ca, hc, us, ul, g, qa, ell, xt, hx, ct, hy)
    for j in range(NB):
        t, s = block_terms(j, ca, g, qa)
        t_ref[j] = t
        scale = scale - s
    s_ref[...] = scale


def last_kernel(me_ref, ca, hc, us, ul, t0, s0, ls_ref, a_ref, b_ref, c_ref, t_ref, s_ref, g, qa, ell, xt, hx, ct, hy, blocks):
    for k, ref in enumerate((a_ref, b_ref, c_ref)):
        for i in range(NSIDE):
            blocks[NSIDE * k + i] = ref[i]
    scale = s0[...] + add_pairs(blocks, 3 * NSIDE, ca, hc, us, ul, g, qa, ell, xt, hx, ct, hy)
    ls = ls_ref[...]
    me = me_ref[0]
    for j in range(NB):
        t, s = block_terms(j, ca, g, qa)
        h = me if j % 2 == 0 else 1 - me
        t_ref[h, j // 2] = (t0[j] + t) / ls
        scale = scale - s
    s_ref[...] = scale


def plane_shift(value, by, swap):
    perm = []
    for y in range(4):
        for core in range(2):
            for x in range(4):
                along_x = (core == 0) != swap
                ty, tx = (y, (x + by) % 4) if along_x else ((y + by) % 4, x)
                perm.append(((y * 2 + core) * 4 + x, (ty * 2 + core) * 4 + tx))
    return lax.ppermute(value, PLANE_AXES, perm)


def pieces(s):
    a = s.astype(BF)
    rest = s - a.astype(F32)
    b = rest.astype(BF)
    c = (rest - b.astype(F32)).astype(BF)
    return jnp.concatenate([jnp.stack([a, b, c]), jnp.zeros((TAIL - 3, D), BF)], 0)


def cost(peers):
    rows = peers * BASE
    return pl.CostEstimate(flops=2 * rows * M * 288, bytes_accessed=2**22, transcendentals=rows * M)


def local(points, adjoint_rows, centers, solution_rows, center_left, center_right, lengthscale):
    ls = lengthscale.reshape(1, D)
    shape = jax.ShapeDtypeStruct
    pp, cb = pl.pallas_call(
        prep_kernel,
        out_shape=[shape((PROWS, D), BF), shape((CROWS, D), BF)],
        in_specs=[VM] * 7,
        out_specs=[VM] * 2,
        name="prep",
    )(points, adjoint_rows.T, centers, solution_rows.T, center_left.T, center_right.T, ls)
    side = [pp] + [plane_shift(pp, by, False) for by in (1, 3, 2)]
    line = jnp.stack(side)
    rest = [plane_shift(line, by, True) for by in (1, 3, 2)]
    cen = lax.all_gather(cb, BLOCK_AXES, axis=0, tiled=False)
    work = [
        pltpu.VMEM((M, D), F32),
        pltpu.VMEM((M, D), F32),
        pltpu.VMEM((32, 2 * D), F32),
        pltpu.VMEM((2, D, NSIDE * PTS), BF),
        pltpu.VMEM((2, 8, NSIDE * PTS), F32),
        pltpu.VMEM((2, D, NSIDE * CTR), BF),
        pltpu.VMEM((2, 8, NSIDE * CTR), F32),
    ]
    state = pl.pallas_call(
        first_kernel,
        out_shape=[
            shape((M, D), BF),
            shape((M, D), F32),
            shape((M, D), BF),
            shape((M, D), BF),
            shape((NB, CTR, D), F32),
            shape((8, D), F32),
        ],
        in_specs=[VM] * 5,
        out_specs=[VM] * 6,
        scratch_shapes=work + [pltpu.VMEM((NSIDE, PROWS, D), BF)],
        compiler_params=PARAMS,
        cost_estimate=cost(NSIDE),
        name="pairs_first",
    )(cen, *side)
    me = lax.axis_index("core").astype(jnp.int32).reshape(1)
    terms, scale = pl.pallas_call(
        last_kernel,
        out_shape=[shape((2, NZ, CTR, D), F32), shape((8, D), F32)],
        in_specs=[SM] + [VM] * 10,
        out_specs=[VM] * 2,
        scratch_shapes=work + [pltpu.VMEM((3 * NSIDE, PROWS, D), BF)],
        compiler_params=PARAMS,
        cost_estimate=cost(3 * NSIDE),
        name="pairs_last",
    )(me, *state, ls, *rest)
    swapped = lax.ppermute(terms[1], "core", [(0, 1), (1, 0)])
    tiny = jnp.broadcast_to(scale[None], (32, 8, D))
    scale = jnp.sum(lax.all_to_all(tiny, SCALE_AXES, 0, 0, tiled=True), (0, 1))
    mine = (terms[0] + swapped).astype(BF)
    chunk = jnp.concatenate([mine, jnp.broadcast_to(pieces(scale)[None], (NZ, TAIL, D))], 1)
    parts = jnp.sum(lax.all_to_all(chunk, CENTER_AXES, 0, 0, tiled=True).astype(F32), 0)
    return parts[0:CTR], jnp.sum(parts[CTR:], 0) / lengthscale


def solution(mesh):
    grid = Mesh(mesh.devices.reshape(SIZES), AXES)
    rows = P(AXES, None)
    return jax.shard_map(
        local,
        mesh=grid,
        in_specs=(rows,) * 6 + (P(),),
        out_specs=(rows, P()),
        check_vma=False,
    )
```

```python
import functools

import jax
import jax.numpy as jnp
from jax import lax
from jax.experimental import pallas as pl
from jax.experimental.pallas import tpu as pltpu
from jax.sharding import Mesh, PartitionSpec as P

BF = jnp.bfloat16
F32 = jnp.float32
AXES = ("zh", "y", "core", "zl", "x")
SIZES = (4, 4, 2, 2, 4)
CENTER_AXES = ("zh", "zl")
PLANE_AXES = ("y", "core", "x")
SCALE_AXES = ("y", "x", "core")
D = 128
R = 32
PTS = 256
CTR = 128
CROWS = CTR + 3 * R
BASE = PTS + CTR
PROWS = BASE + 4 * R
TAIL = 16
NZ = 8
NB = 2 * NZ
NSIDE = 4
SHIFTS = (0, 1, 3, 2)
M = NB * CTR
VM = pl.BlockSpec(memory_space=pltpu.VMEM)
SM = pl.BlockSpec(memory_space=pltpu.SMEM)
PARAMS = pltpu.CompilerParams(vmem_limit_bytes=44 * 2**20)


def dot_nn(a, b):
    return lax.dot_general(a, b, (((1,), (0,)), ((), ())), preferred_element_type=F32)


def fold(v):
    return jnp.sum(v.reshape(v.shape[0] // 8, 8, v.shape[1]), axis=0)


def prep_kernel(x_ref, v_ref, c_ref, s_ref, l_ref, r_ref, ls_ref, pp_ref, cb_ref, lv_ref):
    ls = ls_ref[...]
    x = (x_ref[...].astype(F32) / ls).astype(BF)
    c = (c_ref[...].astype(F32) / ls).astype(BF)
    lt, rt = l_ref[...], r_ref[...]
    pp_ref[...] = jnp.concatenate([x, c, v_ref[:, 0:CTR], v_ref[:, CTR:PTS], rt, lt], 0)
    cb_ref[...] = jnp.concatenate([c, s_ref[...], lt, rt], 0)
    lv_ref[...] = jnp.broadcast_to(ls, lv_ref.shape)


def set_centers(own_ref, oth_ref, ca, hc, us, ul):
    lane = lax.broadcasted_iota(jnp.int32, (CTR, 128), 1)
    for j in range(NB):
        rows = slice(j * CTR, (j + 1) * CTR)
        cen_ref, i = (own_ref, j) if j < NZ else (oth_ref, j - NZ)
        c = cen_ref[i, 0:CTR, :]
        cf = c.astype(F32)
        ca[rows, :] = c
        hc[rows, :] = jnp.broadcast_to(0.5 * jnp.sum(cf * cf, axis=1, keepdims=True), (CTR, 128))
        ut = jnp.concatenate([cen_ref[i, CTR:CROWS, :], jnp.zeros((R, 128), BF)], 0)
        u = ut.astype(F32).T
        us[rows, :] = jnp.where(lane < R, u, 0.0).astype(BF)
        ul[rows, :] = jnp.where((lane >= R) & (lane < 3 * R), u, 0.0).astype(BF)


def turn(rows, xt, hx, slot, at):
    t = rows.astype(F32).T
    cols = slice(at * 128, (at + 1) * 128)
    xt[slot, :, cols] = t.astype(BF)
    hx[slot, :, cols] = jnp.broadcast_to(0.5 * jnp.sum(t * t, axis=0, keepdims=True), (8, 128))


def sweep(x, xt, hx, vt, ca, hc, u_ref, g, qa):
    n = x.shape[0]
    cross = dot_nn(ca[...], xt)
    prod = dot_nn(u_ref[...], vt)
    h = hc[...]
    parts = []
    for k in range(n // 128):
        cols = slice(k * 128, (k + 1) * 128)
        parts.append(jnp.exp((cross[:, cols] - h) - hx[:, cols]) * prod[:, cols])
    w = jnp.concatenate(parts, 1)
    g[...] += dot_nn(w.astype(BF), x)
    s = parts[0]
    for p in parts[1:]:
        s = s + p
    qa[...] += s
    return w


def add_pairs(blocks, count, ca, hc, us, ul, g, qa, ell, xt, hx, ct, hy):
    g[...] = jnp.zeros_like(g)
    qa[...] = jnp.zeros_like(qa)
    ell[...] = jnp.zeros_like(ell)
    steps = count // NSIDE

    def turn_points(a, slot):
        for k in range(NSIDE):
            turn(blocks[NSIDE * a + k, 0:128, :], xt, hx, slot, 2 * k)
            turn(blocks[NSIDE * a + k, 128:PTS, :], xt, hx, slot, 2 * k + 1)

    def turn_centers(a, slot):
        for k in range(NSIDE):
            turn(blocks[NSIDE * a + k, PTS:BASE, :], ct, hy, slot, k)

    def points_step(a, carry):
        ids = [NSIDE * a + k for k in range(NSIDE)]
        slot = lax.rem(a, 2)
        x = jnp.concatenate([blocks[i, 0:PTS, :] for i in ids], 0)
        vt = jnp.concatenate(
            [blocks[i, BASE + k * R : BASE + (k + 1) * R, :] for i in ids for k in (0, 1)], 1
        )
        vt = jnp.concatenate([vt, jnp.zeros((3 * R, NSIDE * PTS), BF)], 0)
        w = sweep(x, xt[slot], hx[slot, 0:1, :], vt, ca, hc, us, g, qa)
        if steps > 1:
            turn_points(lax.min(a + 1, steps - 1), 1 - slot)
        rowsum = fold(w)
        r1 = rowsum.astype(BF)
        rest = rowsum - r1.astype(F32)
        r2 = rest.astype(BF)
        r3 = (rest - r2.astype(F32)).astype(BF)
        xf = x.astype(F32)
        xsq = xf * xf
        xh = xsq.astype(BF)
        xl = (xsq - xh.astype(F32)).astype(BF)
        ell[...] += dot_nn(
            jnp.concatenate([r1, r2, r3, jnp.zeros_like(r1)], 0), jnp.concatenate([xh, xl], 1)
        )
        return carry

    def centers_step(a, carry):
        ids = [NSIDE * a + k for k in range(NSIDE)]
        slot = lax.rem(a, 2)
        c = jnp.concatenate([blocks[i, PTS:BASE, :] for i in ids], 0)
        z = jnp.zeros((R, NSIDE * CTR), BF)
        vc = jnp.concatenate([blocks[i, BASE + 2 * R : PROWS, :] for i in ids], 1)
        sweep(c, ct[slot], hy[slot, 0:1, :], jnp.concatenate([z, vc, z], 0), ca, hc, ul, g, qa)
        if steps > 1:
            turn_centers(lax.min(a + 1, steps - 1), 1 - slot)
        return carry

    turn_points(0, 0)
    lax.fori_loop(0, steps, points_step, 0)
    e = ell[...]
    e = e[:, 0:128] + e[:, 128:256]
    scale = e[0:8] + e[8:16] + e[16:24]
    for j in range(NB):
        rows = slice(j * CTR, (j + 1) * CTR)
        scale = scale - fold(ca[rows, :].astype(F32) * g[rows, :])
    turn_centers(0, 0)
    lax.fori_loop(0, steps, centers_step, 0)
    return scale


def block_terms(j, ca, g, qa):
    rows = slice(j * CTR, (j + 1) * CTR)
    c = ca[rows, :].astype(F32)
    q = jnp.sum(qa[rows, :], axis=1, keepdims=True)
    t = g[rows, :] - q * c
    return t, fold(c * t)


def first_kernel(own_ref, oth_ref, a_ref, b_ref, c_ref, d_ref, ca, hc, us, ul, t_ref, s_ref, g, qa, ell, xt, hx, ct, hy, blocks):
    set_centers(own_ref, oth_ref, ca, hc, us, ul)
    for k, ref in enumerate((a_ref, b_ref, c_ref, d_ref)):
        blocks[k] = ref[...]
    scale = add_pairs(blocks, NSIDE, ca, hc, us, ul, g, qa, ell, xt, hx, ct, hy)
    for j in range(NB):
        t, s = block_terms(j, ca, g, qa)
        t_ref[j] = t
        scale = scale - s
    s_ref[...] = scale


def last_kernel(at_ref, ca, hc, us, ul, t0, s0, ls_ref, a_ref, b_ref, c_ref, t_ref, s_ref, g, qa, ell, xt, hx, ct, hy, blocks):
    for k, ref in enumerate((a_ref, b_ref, c_ref)):
        for i in range(NSIDE):
            blocks[NSIDE * k + i] = ref[i]
    scale = s0[...] + add_pairs(blocks, 3 * NSIDE, ca, hc, us, ul, g, qa, ell, xt, hx, ct, hy)
    ls = ls_ref[0:1, :]
    zh, zl = at_ref[0], at_ref[1]
    for j in range(NB):
        t, s = block_terms(j, ca, g, qa)
        h, i = divmod(j, NZ)
        place = lax.rem(zh + 4 - SHIFTS[i // 2], 4) * 2 + (zl if i % 2 == 0 else 1 - zl)
        t_ref[h, place] = (t0[j] + t) / ls
        scale = scale - s
    s_ref[...] = scale


def shifted(value, axis, by):
    n = dict(zip(AXES, SIZES))[axis]
    return lax.ppermute(value, axis, [(i, (i + by) % n) for i in range(n)])


def plane_shift(value, by, swap):
    perm = []
    for y in range(4):
        for core in range(2):
            for x in range(4):
                along_x = (core == 0) != swap
                ty, tx = (y, (x + by) % 4) if along_x else ((y + by) % 4, x)
                perm.append(((y * 2 + core) * 4 + x, (ty * 2 + core) * 4 + tx))
    return lax.ppermute(value, PLANE_AXES, perm)


def pieces(s):
    a = s.astype(BF)
    rest = s - a.astype(F32)
    b = rest.astype(BF)
    c = (rest - b.astype(F32)).astype(BF)
    return jnp.concatenate([jnp.stack([a, b, c]), jnp.zeros((TAIL - 3, D), BF)], 0)


def cost(peers):
    rows = peers * BASE
    return pl.CostEstimate(flops=2 * rows * M * 288, bytes_accessed=2**22, transcendentals=rows * M)


def local(points, adjoint_rows, centers, solution_rows, center_left, center_right, lengthscale):
    ls = lengthscale.reshape(1, D)
    shape = jax.ShapeDtypeStruct
    pp, cb, lv = pl.pallas_call(
        prep_kernel,
        out_shape=[shape((PROWS, D), BF), shape((CROWS, D), BF), shape((8, D), F32)],
        in_specs=[VM] * 7,
        out_specs=[VM] * 3,
        name="prep",
    )(points, adjoint_rows.T, centers, solution_rows.T, center_left.T, center_right.T, ls)
    side = [pp] + [plane_shift(pp, by, False) for by in (1, 3, 2)]
    two = jnp.stack([cb, shifted(cb, "zl", 1)])
    line = jnp.stack(side)
    rest = [plane_shift(line, by, True) for by in (1, 3, 2)]
    own = jnp.concatenate([two] + [shifted(two, "zh", by) for by in SHIFTS[1:]], 0)
    oth = shifted(own, "core", 1)
    work = [
        pltpu.VMEM((M, D), F32),
        pltpu.VMEM((M, D), F32),
        pltpu.VMEM((32, 2 * D), F32),
        pltpu.VMEM((2, D, NSIDE * PTS), BF),
        pltpu.VMEM((2, 8, NSIDE * PTS), F32),
        pltpu.VMEM((2, D, NSIDE * CTR), BF),
        pltpu.VMEM((2, 8, NSIDE * CTR), F32),
    ]
    state = pl.pallas_call(
        first_kernel,
        out_shape=[
            shape((M, D), BF),
            shape((M, D), F32),
            shape((M, D), BF),
            shape((M, D), BF),
            shape((NB, CTR, D), F32),
            shape((8, D), F32),
        ],
        in_specs=[VM] * 6,
        out_specs=[VM] * 6,
        scratch_shapes=work + [pltpu.VMEM((NSIDE, PROWS, D), BF)],
        compiler_params=PARAMS,
        cost_estimate=pl.CostEstimate(flops=1, bytes_accessed=1, transcendentals=0),
        name="pairs_first",
    )(own, oth, *side)
    at = jnp.stack([lax.axis_index("zh"), lax.axis_index("zl")]).astype(jnp.int32)
    terms, scale = pl.pallas_call(
        last_kernel,
        out_shape=[shape((2, NZ, CTR, D), F32), shape((8, D), F32)],
        in_specs=[SM] + [VM] * 10,
        out_specs=[VM] * 2,
        scratch_shapes=work + [pltpu.VMEM((3 * NSIDE, PROWS, D), BF)],
        compiler_params=PARAMS,
        cost_estimate=cost(3 * NSIDE),
        name="pairs_last",
    )(at, *state, lv, *rest)
    swapped = shifted(terms[1], "core", 1)
    tiny = jnp.broadcast_to(scale[None], (32, 8, D))
    scale = jnp.sum(lax.all_to_all(tiny, SCALE_AXES, 0, 0, tiled=True), (0, 1))
    mine = (terms[0] + swapped).astype(BF)
    chunk = jnp.concatenate([mine, jnp.broadcast_to(pieces(scale)[None], (NZ, TAIL, D))], 1)
    parts = lax.all_to_all(chunk, CENTER_AXES, 0, 0, tiled=True)
    total = jnp.sum(parts[:, 0:CTR].astype(F32), 0)
    return total, jnp.sum(parts[:, CTR:].astype(F32), (0, 1)) / lv[0]


def solution(mesh):
    grid = Mesh(mesh.devices.reshape(SIZES), AXES)
    rows = P(AXES, None)
    return jax.shard_map(
        local,
        mesh=grid,
        in_specs=(rows,) * 6 + (P(),),
        out_specs=(rows, P()),
        check_vma=False,
    )
```

```python
import functools

import jax
import jax.numpy as jnp
from jax import lax
from jax.experimental import pallas as pl
from jax.experimental.pallas import tpu as pltpu
from jax.sharding import Mesh, PartitionSpec as P

BF = jnp.bfloat16
F32 = jnp.float32
AXES = ("zh", "y", "core", "zl", "x")
SIZES = (4, 4, 2, 2, 4)
CENTER_AXES = ("zh", "zl")
PLANE_AXES = ("y", "core", "x")
SCALE_AXES = ("y", "x", "core")
D = 128
R = 32
PTS = 256
CTR = 128
CROWS = CTR + 3 * R
BASE = PTS + CTR
PROWS = BASE + 4 * R
TAIL = 16
NZ = 8
NB = 2 * NZ
NSIDE = 4
SHIFTS = (0, 1, 3, 2)
SPAN = 1024
PER = {4: 4, 12: 12}
M = NB * CTR
VM = pl.BlockSpec(memory_space=pltpu.VMEM)
SM = pl.BlockSpec(memory_space=pltpu.SMEM)
PARAMS = pltpu.CompilerParams(vmem_limit_bytes=44 * 2**20)


def dot_nn(a, b):
    return lax.dot_general(a, b, (((1,), (0,)), ((), ())), preferred_element_type=F32)


def fold(v):
    return jnp.sum(v.reshape(v.shape[0] // 8, 8, v.shape[1]), axis=0)


def prep_kernel(x_ref, v_ref, c_ref, s_ref, l_ref, r_ref, ls_ref, pp_ref, cb_ref, lv_ref):
    ls = ls_ref[...]
    x = (x_ref[...].astype(F32) / ls).astype(BF)
    c = (c_ref[...].astype(F32) / ls).astype(BF)
    lt, rt = l_ref[...], r_ref[...]
    pp_ref[...] = jnp.concatenate([x, c, v_ref[:, 0:CTR], v_ref[:, CTR:PTS], rt, lt], 0)
    cb_ref[...] = jnp.concatenate([c, s_ref[...], lt, rt], 0)
    lv_ref[...] = jnp.broadcast_to(ls, lv_ref.shape)


def set_centers(held, ct, hc, ut):
    for j in range(NB):
        h, i = divmod(j, NZ)
        ref, i = (held[2 * h], i) if i < 2 else (held[2 * h + 1], i - 2)
        cols = slice(j * CTR, (j + 1) * CTR)
        t = ref[i, 0:CTR, :].astype(F32).T
        ct[:, cols] = t.astype(BF)
        hc[:, cols] = jnp.broadcast_to(0.5 * jnp.sum(t * t, axis=0, keepdims=True), (8, CTR))
        ut[0 : 3 * R, cols] = ref[i, CTR:CROWS, :]
        ut[3 * R : D, cols] = jnp.zeros((R, CTR), BF)


def turn(rows, vrows, first, xt, hx, vs, slot, at):
    span = slice(at * 128, (at + 1) * 128)
    f = rows.astype(F32)
    xt[slot, :, span] = f.T.astype(BF)
    hx[slot, span, :] = jnp.broadcast_to(0.5 * jnp.sum(f * f, axis=1, keepdims=True), (128, 128))
    above = [jnp.zeros((first, 128), F32)] if first else []
    below = jnp.zeros((128 - first - vrows.shape[0], 128), F32)
    vs[slot, span, :] = jnp.concatenate(above + [vrows.astype(F32), below], 0).T.astype(BF)


def sweep(x, xt, hx, vs, ct, hc, ut, gt, qt, want_rows):
    n = x.shape[0]
    rows = None
    for m in range(0, M, SPAN):
        cols = slice(m, m + SPAN)
        cross = dot_nn(x, ct[:, cols])
        prod = dot_nn(vs, ut[:, cols])
        parts = []
        for k in range(SPAN // 128):
            part = slice(k * 128, (k + 1) * 128)
            h = hc[0:1, m + k * 128 : m + (k + 1) * 128]
            parts.append(jnp.exp((cross[:, part] - hx) - h) * prod[:, part])
        w = jnp.concatenate(parts, 1)
        gt[:, cols] += dot_nn(xt, w.astype(BF))
        qt[:, cols] += fold(w)
        if want_rows:
            for p in parts:
                rows = p if rows is None else rows + p
    return rows


def add_pairs(blocks, count, ct, hc, ut, gt, qt, xt, hx, vs, yt, hy, us):
    gt[...] = jnp.zeros_like(gt)
    qt[...] = jnp.zeros_like(qt)
    per = PER[count]
    steps, csteps = count // NSIDE, count // per

    def turn_points(a, slot):
        for k in range(2 * NSIDE):
            i, h = NSIDE * a + k // 2, k % 2
            vrows = blocks[i, BASE + h * R : BASE + (h + 1) * R, :]
            turn(blocks[i, h * 128 : (h + 1) * 128, :], vrows, 0, xt, hx, vs, slot, k)

    def turn_centers(a, slot):
        for k in range(per):
            i = per * a + k
            turn(blocks[i, PTS:BASE, :], blocks[i, BASE + 2 * R : PROWS, :], R, yt, hy, us, slot, k)

    def points_step(a, ell):
        slot = lax.rem(a, 2)
        x = jnp.concatenate([blocks[NSIDE * a + k, 0:PTS, :] for k in range(NSIDE)], 0)
        rows = sweep(x, xt[slot], hx[slot], vs[slot], ct, hc, ut, gt, qt, True)
        if steps > 1:
            turn_points(lax.min(a + 1, steps - 1), 1 - slot)
        xf = x.astype(F32)
        return ell + fold(jnp.sum(rows, axis=1, keepdims=True) * (xf * xf))

    def centers_step(a, carry):
        slot = lax.rem(a, 2)
        c = jnp.concatenate([blocks[per * a + k, PTS:BASE, :] for k in range(per)], 0)
        sweep(c, yt[slot], hy[slot], us[slot], ct, hc, ut, gt, qt, False)
        if csteps > 1:
            turn_centers(lax.min(a + 1, csteps - 1), 1 - slot)
        return carry

    turn_points(0, 0)
    ell = lax.fori_loop(0, steps, points_step, jnp.zeros((8, D), F32))
    both = jnp.zeros((D, CTR), F32)
    for j in range(NB):
        cols = slice(j * CTR, (j + 1) * CTR)
        both = both + ct[:, cols].astype(F32) * gt[:, cols]
    turn_centers(0, 0)
    lax.fori_loop(0, csteps, centers_step, 0)
    return ell, both


def block_terms(j, ct, gt, qt):
    cols = slice(j * CTR, (j + 1) * CTR)
    c = ct[:, cols].astype(F32)
    q = jnp.sum(qt[:, cols], axis=0, keepdims=True)
    t = gt[:, cols] - q * c
    return t, c * t


def first_kernel(h0, h1, h2, h3, a_ref, b_ref, c_ref, d_ref, lv_ref, ct, hc, ut, t_ref, s_ref, gt, qt, *work):
    set_centers((h0, h1, h2, h3), ct, hc, ut)
    blocks = work[-1]
    for k, ref in enumerate((a_ref, b_ref, c_ref, d_ref)):
        blocks[k] = ref[...]
    ell, both = add_pairs(blocks, NSIDE, ct, hc, ut, gt, qt, *work[:-1])
    for j in range(NB):
        t, s = block_terms(j, ct, gt, qt)
        t_ref[:, j * CTR : (j + 1) * CTR] = t
        both = both + s
    s_ref[0:8, :] = ell - fold(both.T)
    s_ref[8:16, :] = lv_ref[...]


def last_kernel(at_ref, ct, hc, ut, t0, s0, a_ref, b_ref, c_ref, t_ref, s_ref, gt, qt, *work):
    blocks = work[-1]
    for k, ref in enumerate((a_ref, b_ref, c_ref)):
        for i in range(NSIDE):
            blocks[NSIDE * k + i] = ref[i]
    ell, both = add_pairs(blocks, 3 * NSIDE, ct, hc, ut, gt, qt, *work[:-1])
    inv = 1.0 / s0[8:9, :]
    zh, zl = at_ref[0], at_ref[1]
    for j in range(NB):
        t, s = block_terms(j, ct, gt, qt)
        both = both + s
        h, i = divmod(j, NZ)
        place = lax.rem(zh + 4 - SHIFTS[i // 2], 4) * 2 + (zl if i % 2 == 0 else 1 - zl)
        t_ref[h, place] = (t0[:, j * CTR : (j + 1) * CTR] + t).T * inv
    scale = jnp.sum(s0[0:8, :] + ell - fold(both.T), axis=0, keepdims=True)
    s_ref[...] = jnp.broadcast_to(scale[None], s_ref.shape)


def shifted(value, axis, by):
    n = dict(zip(AXES, SIZES))[axis]
    return lax.ppermute(value, axis, [(i, (i + by) % n) for i in range(n)])


def plane_shift(value, by, swap):
    perm = []
    for y in range(4):
        for core in range(2):
            for x in range(4):
                along_x = (core == 0) != swap
                ty, tx = (y, (x + by) % 4) if along_x else ((y + by) % 4, x)
                perm.append(((y * 2 + core) * 4 + x, (ty * 2 + core) * 4 + tx))
    return lax.ppermute(value, PLANE_AXES, perm)


def pieces(s):
    a = s.astype(BF)
    rest = s - a.astype(F32)
    b = rest.astype(BF)
    c = (rest - b.astype(F32)).astype(BF)
    return jnp.concatenate([jnp.stack([a, b, c]), jnp.zeros((TAIL - 3, D), BF)], 0)


def cost(peers):
    rows = peers * BASE
    return pl.CostEstimate(flops=2 * rows * M * 288, bytes_accessed=2**22, transcendentals=rows * M)


def work_space(count):
    n, nc = NSIDE * PTS, PER[count] * CTR
    return [
        pltpu.VMEM((D, M), F32),
        pltpu.VMEM((8, M), F32),
        pltpu.VMEM((2, D, n), BF),
        pltpu.VMEM((2, n, 128), F32),
        pltpu.VMEM((2, n, 128), BF),
        pltpu.VMEM((2, D, nc), BF),
        pltpu.VMEM((2, nc, 128), F32),
        pltpu.VMEM((2, nc, 128), BF),
        pltpu.VMEM((count, PROWS, D), BF),
    ]


def first_call(*args):
    shape = jax.ShapeDtypeStruct
    return pl.pallas_call(
        first_kernel,
        out_shape=[
            shape((D, M), BF),
            shape((8, M), F32),
            shape((D, M), BF),
            shape((D, M), F32),
            shape((16, D), F32),
        ],
        in_specs=[VM] * 9,
        out_specs=[VM] * 5,
        scratch_shapes=work_space(NSIDE),
        compiler_params=PARAMS,
        cost_estimate=pl.CostEstimate(flops=1, bytes_accessed=1, transcendentals=0),
        name="pairs_first",
    )(*args)


def last_call(*args):
    shape = jax.ShapeDtypeStruct
    return pl.pallas_call(
        last_kernel,
        out_shape=[shape((2, NZ, CTR, D), F32), shape((32, 1, D), F32)],
        in_specs=[SM] + [VM] * 8,
        out_specs=[VM] * 2,
        scratch_shapes=work_space(3 * NSIDE),
        compiler_params=PARAMS,
        cost_estimate=cost(3 * NSIDE),
        name="pairs_last",
    )(*args)


def local(points, adjoint_rows, centers, solution_rows, center_left, center_right, lengthscale):
    ls = lengthscale.reshape(1, D)
    shape = jax.ShapeDtypeStruct
    pp, cb, lv = pl.pallas_call(
        prep_kernel,
        out_shape=[shape((PROWS, D), BF), shape((CROWS, D), BF), shape((8, D), F32)],
        in_specs=[VM] * 7,
        out_specs=[VM] * 3,
        name="prep",
    )(points, adjoint_rows.T, centers, solution_rows.T, center_left.T, center_right.T, ls)
    side = [pp] + [plane_shift(pp, by, False) for by in (1, 3, 2)]
    two = jnp.stack([cb, shifted(cb, "zl", 1)])
    line = jnp.stack(side)
    rest = [plane_shift(line, by, True) for by in (1, 3, 2)]
    two_other = shifted(two, "core", 1)
    six = jnp.concatenate([shifted(two, "zh", by) for by in SHIFTS[1:]], 0)
    held = (two, six, two_other, shifted(six, "core", 1))
    at = jnp.stack([lax.axis_index("zh"), lax.axis_index("zl")]).astype(jnp.int32)
    terms, scale = last_call(at, *first_call(*held, *side, lv), *rest)
    swapped = shifted(terms[1], "core", 1)
    scale = jnp.sum(lax.all_to_all(scale, SCALE_AXES, 0, 0, tiled=True), (0, 1))
    mine = (terms[0] + swapped).astype(BF)
    chunk = jnp.concatenate([mine, jnp.broadcast_to(pieces(scale)[None], (NZ, TAIL, D))], 1)
    parts = lax.all_to_all(chunk, CENTER_AXES, 0, 0, tiled=True)
    total = jnp.sum(parts[:, 0:CTR].astype(F32), 0)
    return total, jnp.sum(parts[:, CTR:].astype(F32), (0, 1)) / lv[0]


def solution(mesh):
    grid = Mesh(mesh.devices.reshape(SIZES), AXES)
    rows = P(AXES, None)
    return jax.shard_map(
        local,
        mesh=grid,
        in_specs=(rows,) * 6 + (P(),),
        out_specs=(rows, P()),
        check_vma=False,
    )
```

```python
import functools

import jax
import jax.numpy as jnp
from jax import lax
from jax.experimental import pallas as pl
from jax.experimental.pallas import tpu as pltpu
from jax.sharding import Mesh, PartitionSpec as P

BF = jnp.bfloat16
F32 = jnp.float32
AXES = ("zh", "y", "core", "zl", "x")
SIZES = (4, 4, 2, 2, 4)
CENTER_AXES = ("zh", "zl")
PLANE_AXES = ("y", "core", "x")
SCALE_AXES = ("y", "x", "core")
D = 128
R = 32
PTS = 256
CTR = 128
CROWS = CTR + 3 * R
BASE = PTS + CTR
PROWS = BASE + 4 * R
TAIL = 16
NZ = 8
NB = 2 * NZ
NSIDE = 4
SHIFTS = (0, 1, 3, 2)
SPAN = 1024
M = NB * CTR
VM = pl.BlockSpec(memory_space=pltpu.VMEM)
SM = pl.BlockSpec(memory_space=pltpu.SMEM)
PARAMS = pltpu.CompilerParams(vmem_limit_bytes=44 * 2**20)


def dot_nn(a, b):
    return lax.dot_general(a, b, (((1,), (0,)), ((), ())), preferred_element_type=F32)


def fold(v):
    return jnp.sum(v.reshape(v.shape[0] // 8, 8, v.shape[1]), axis=0)


def prep_kernel(x_ref, v_ref, c_ref, s_ref, l_ref, r_ref, ls_ref, pp_ref, cb_ref, lv_ref):
    ls = ls_ref[...]
    x = (x_ref[...].astype(F32) / ls).astype(BF)
    c = (c_ref[...].astype(F32) / ls).astype(BF)
    lt, rt = l_ref[...], r_ref[...]
    pp_ref[...] = jnp.concatenate([x, c, v_ref[:, 0:CTR], v_ref[:, CTR:PTS], rt, lt], 0)
    cb_ref[...] = jnp.concatenate([c, s_ref[...], lt, rt], 0)
    lv_ref[...] = jnp.broadcast_to(ls, lv_ref.shape)


def set_centers(held, ct, hc, ut):
    for j in range(NB):
        h, i = divmod(j, NZ)
        ref, i = (held[2 * h], i) if i < 2 else (held[2 * h + 1], i - 2)
        cols = slice(j * CTR, (j + 1) * CTR)
        t = ref[i, 0:CTR, :].astype(F32).T
        ct[:, cols] = t.astype(BF)
        hc[:, cols] = jnp.broadcast_to(0.5 * jnp.sum(t * t, axis=0, keepdims=True), (8, CTR))
        ut[0 : 3 * R, cols] = ref[i, CTR:CROWS, :]
        ut[3 * R : D, cols] = jnp.zeros((R, CTR), BF)


def turn(rows, vrows, first, xt, hx, vs, slot, at):
    span = slice(at * 128, (at + 1) * 128)
    f = rows.astype(F32)
    xt[slot, :, span] = f.T.astype(BF)
    hx[slot, span, :] = jnp.broadcast_to(0.5 * jnp.sum(f * f, axis=1, keepdims=True), (128, 128))
    above = [jnp.zeros((first, 128), F32)] if first else []
    below = jnp.zeros((128 - first - vrows.shape[0], 128), F32)
    vs[slot, span, :] = jnp.concatenate(above + [vrows.astype(F32), below], 0).T.astype(BF)


def sweep(x, xt, hx, vs, ct, hc, ut, gt, qt, want_rows):
    n = x.shape[0]
    rows = None
    for m in range(0, M, SPAN):
        cols = slice(m, m + SPAN)
        cross = dot_nn(x, ct[:, cols])
        prod = dot_nn(vs, ut[:, cols])
        parts = []
        for k in range(SPAN // 128):
            part = slice(k * 128, (k + 1) * 128)
            h = hc[0:1, m + k * 128 : m + (k + 1) * 128]
            parts.append(jnp.exp((cross[:, part] - hx) - h) * prod[:, part])
        w = jnp.concatenate(parts, 1)
        gt[:, cols] += dot_nn(xt, w.astype(BF))
        qt[:, cols] += fold(w)
        if want_rows:
            for p in parts:
                rows = p if rows is None else rows + p
    return rows


def add_pairs(blocks, count, ct, hc, ut, gt, qt, xt, hx, vs, yt, hy, us):
    gt[...] = jnp.zeros_like(gt)
    qt[...] = jnp.zeros_like(qt)
    steps = count // NSIDE

    def turn_points(a, slot):
        for k in range(2 * NSIDE):
            i, h = NSIDE * a + k // 2, k % 2
            vrows = blocks[i, BASE + h * R : BASE + (h + 1) * R, :]
            turn(blocks[i, h * 128 : (h + 1) * 128, :], vrows, 0, xt, hx, vs, slot, k)

    def turn_centers(a):
        for k in range(NSIDE):
            i = NSIDE * a + k
            turn(blocks[i, PTS:BASE, :], blocks[i, BASE + 2 * R : PROWS, :], R, yt, hy, us, a, k)

    def points_step(a, ell):
        slot = lax.rem(a, 2)
        x = jnp.concatenate([blocks[NSIDE * a + k, 0:PTS, :] for k in range(NSIDE)], 0)
        rows = sweep(x, xt[slot], hx[slot], vs[slot], ct, hc, ut, gt, qt, True)
        if steps > 1:
            turn_points(lax.min(a + 1, steps - 1), 1 - slot)
        turn_centers(a)
        xf = x.astype(F32)
        return ell + fold(jnp.sum(rows, axis=1, keepdims=True) * (xf * xf))

    turn_points(0, 0)
    ell = lax.fori_loop(0, steps, points_step, jnp.zeros((8, D), F32))
    both = jnp.zeros((D, CTR), F32)
    for j in range(NB):
        cols = slice(j * CTR, (j + 1) * CTR)
        both = both + ct[:, cols].astype(F32) * gt[:, cols]
    c = jnp.concatenate([blocks[i, PTS:BASE, :] for i in range(count)], 0)
    yts, hys, uss = (
        jnp.concatenate([ref[a] for a in range(steps)], axis) for ref, axis in ((yt, 1), (hy, 0), (us, 0))
    )
    sweep(c, yts, hys, uss, ct, hc, ut, gt, qt, False)
    return ell, both


def block_terms(j, ct, gt, qt):
    cols = slice(j * CTR, (j + 1) * CTR)
    c = ct[:, cols].astype(F32)
    q = jnp.sum(qt[:, cols], axis=0, keepdims=True)
    t = gt[:, cols] - q * c
    return t, c * t


def first_kernel(h0, h1, h2, h3, a_ref, b_ref, c_ref, d_ref, lv_ref, ct, hc, ut, t_ref, s_ref, gt, qt, *work):
    set_centers((h0, h1, h2, h3), ct, hc, ut)
    blocks = work[-1]
    for k, ref in enumerate((a_ref, b_ref, c_ref, d_ref)):
        blocks[k] = ref[...]
    ell, both = add_pairs(blocks, NSIDE, ct, hc, ut, gt, qt, *work[:-1])
    for j in range(NB):
        t, s = block_terms(j, ct, gt, qt)
        t_ref[:, j * CTR : (j + 1) * CTR] = t
        both = both + s
    s_ref[0:8, :] = ell - fold(both.T)
    s_ref[8:16, :] = lv_ref[...]


def middle_kernel(ct, hc, ut, t0, s0, a_ref, b_ref, t_ref, s_ref, gt, qt, *work):
    blocks = work[-1]
    for k, ref in enumerate((a_ref, b_ref)):
        for i in range(NSIDE):
            blocks[NSIDE * k + i] = ref[i]
    ell, both = add_pairs(blocks, 2 * NSIDE, ct, hc, ut, gt, qt, *work[:-1])
    for j in range(NB):
        cols = slice(j * CTR, (j + 1) * CTR)
        t, s = block_terms(j, ct, gt, qt)
        t_ref[:, cols] = t0[:, cols] + t
        both = both + s
    s_ref[0:8, :] = s0[0:8, :] + ell - fold(both.T)
    s_ref[8:16, :] = s0[8:16, :]


def last_kernel(at_ref, ct, hc, ut, t0, s0, a_ref, t_ref, s_ref, gt, qt, *work):
    blocks = work[-1]
    for i in range(NSIDE):
        blocks[i] = a_ref[i]
    ell, both = add_pairs(blocks, NSIDE, ct, hc, ut, gt, qt, *work[:-1])
    inv = 1.0 / s0[8:9, :]
    zh, zl = at_ref[0], at_ref[1]
    for j in range(NB):
        t, s = block_terms(j, ct, gt, qt)
        both = both + s
        h, i = divmod(j, NZ)
        place = lax.rem(zh + 4 - SHIFTS[i // 2], 4) * 2 + (zl if i % 2 == 0 else 1 - zl)
        t_ref[h, place] = (t0[:, j * CTR : (j + 1) * CTR] + t).T * inv
    scale = jnp.sum(s0[0:8, :] + ell - fold(both.T), axis=0, keepdims=True)
    s_ref[...] = jnp.broadcast_to(scale[None], s_ref.shape)


def shifted(value, axis, by):
    n = dict(zip(AXES, SIZES))[axis]
    return lax.ppermute(value, axis, [(i, (i + by) % n) for i in range(n)])


def plane_shift(value, by, swap):
    perm = []
    for y in range(4):
        for core in range(2):
            for x in range(4):
                along_x = (core == 0) != swap
                ty, tx = (y, (x + by) % 4) if along_x else ((y + by) % 4, x)
                perm.append(((y * 2 + core) * 4 + x, (ty * 2 + core) * 4 + tx))
    return lax.ppermute(value, PLANE_AXES, perm)


def pieces(s):
    a = s.astype(BF)
    rest = s - a.astype(F32)
    b = rest.astype(BF)
    c = (rest - b.astype(F32)).astype(BF)
    return jnp.concatenate([jnp.stack([a, b, c]), jnp.zeros((TAIL - 3, D), BF)], 0)


def cost(peers):
    rows = peers * BASE
    return pl.CostEstimate(flops=2 * rows * M * 288, bytes_accessed=2**22, transcendentals=rows * M)


def work_space(count):
    n, nc, steps = NSIDE * PTS, NSIDE * CTR, count // NSIDE
    return [
        pltpu.VMEM((D, M), F32),
        pltpu.VMEM((8, M), F32),
        pltpu.VMEM((2, D, n), BF),
        pltpu.VMEM((2, n, 128), F32),
        pltpu.VMEM((2, n, 128), BF),
        pltpu.VMEM((steps, D, nc), BF),
        pltpu.VMEM((steps, nc, 128), F32),
        pltpu.VMEM((steps, nc, 128), BF),
        pltpu.VMEM((count, PROWS, D), BF),
    ]


def first_call(*args):
    shape = jax.ShapeDtypeStruct
    return pl.pallas_call(
        first_kernel,
        out_shape=[
            shape((D, M), BF),
            shape((8, M), F32),
            shape((D, M), BF),
            shape((D, M), F32),
            shape((16, D), F32),
        ],
        in_specs=[VM] * 9,
        out_specs=[VM] * 5,
        scratch_shapes=work_space(NSIDE),
        compiler_params=PARAMS,
        cost_estimate=pl.CostEstimate(flops=1, bytes_accessed=1, transcendentals=0),
        name="pairs_first",
    )(*args)


def middle_call(*args):
    shape = jax.ShapeDtypeStruct
    return pl.pallas_call(
        middle_kernel,
        out_shape=[shape((D, M), F32), shape((16, D), F32)],
        in_specs=[VM] * 7,
        out_specs=[VM] * 2,
        scratch_shapes=work_space(2 * NSIDE),
        compiler_params=PARAMS,
        cost_estimate=pl.CostEstimate(flops=1, bytes_accessed=1, transcendentals=0),
        name="pairs_middle",
    )(*args)


def last_call(*args):
    shape = jax.ShapeDtypeStruct
    return pl.pallas_call(
        last_kernel,
        out_shape=[shape((2, NZ, CTR, D), F32), shape((32, 1, D), F32)],
        in_specs=[SM] + [VM] * 6,
        out_specs=[VM] * 2,
        scratch_shapes=work_space(NSIDE),
        compiler_params=PARAMS,
        cost_estimate=cost(NSIDE),
        name="pairs_last",
    )(*args)


def local(points, adjoint_rows, centers, solution_rows, center_left, center_right, lengthscale):
    ls = lengthscale.reshape(1, D)
    shape = jax.ShapeDtypeStruct
    pp, cb, lv = pl.pallas_call(
        prep_kernel,
        out_shape=[shape((PROWS, D), BF), shape((CROWS, D), BF), shape((8, D), F32)],
        in_specs=[VM] * 7,
        out_specs=[VM] * 3,
        name="prep",
    )(points, adjoint_rows.T, centers, solution_rows.T, center_left.T, center_right.T, ls)
    side = [pp] + [plane_shift(pp, by, False) for by in (1, 3, 2)]
    two = jnp.stack([cb, shifted(cb, "zl", 1)])
    line = jnp.stack(side)
    rest = [plane_shift(line, by, True) for by in (1, 3, 2)]
    two_other = shifted(two, "core", 1)
    six = jnp.concatenate([shifted(two, "zh", by) for by in SHIFTS[1:]], 0)
    held = (two, six, two_other, shifted(six, "core", 1))
    at = jnp.stack([lax.axis_index("zh"), lax.axis_index("zl")]).astype(jnp.int32)
    state = list(first_call(*held, *side, lv))
    state[3:5] = middle_call(*state, *rest[1:])
    terms, scale = last_call(at, *state, rest[0])
    swapped = shifted(terms[1], "core", 1)
    scale = jnp.sum(lax.all_to_all(scale, SCALE_AXES, 0, 0, tiled=True), (0, 1))
    mine = (terms[0] + swapped).astype(BF)
    chunk = jnp.concatenate([mine, jnp.broadcast_to(pieces(scale)[None], (NZ, TAIL, D))], 1)
    parts = lax.all_to_all(chunk, CENTER_AXES, 0, 0, tiled=True)
    total = jnp.sum(parts[:, 0:CTR].astype(F32), 0)
    return total, jnp.sum(parts[:, CTR:].astype(F32), (0, 1)) / lv[0]


def solution(mesh):
    grid = Mesh(mesh.devices.reshape(SIZES), AXES)
    rows = P(AXES, None)
    return jax.shard_map(
        local,
        mesh=grid,
        in_specs=(rows,) * 6 + (P(),),
        out_specs=(rows, P()),
        check_vma=False,
    )
```

```python
import functools

import jax
import jax.numpy as jnp
from jax import lax
from jax.experimental import pallas as pl
from jax.experimental.pallas import tpu as pltpu
from jax.sharding import Mesh, PartitionSpec as P

BF = jnp.bfloat16
F32 = jnp.float32
AXES = ("zh", "y", "core", "zl", "x")
SIZES = (4, 4, 2, 2, 4)
PLANE_AXES = ("y", "core", "x")
SCALE_AXES = ("y", "x", "core", "zl")
D = 128
R = 32
PTS = 256
CTR = 128
CROWS = CTR + 3 * R
BASE = PTS + CTR
PROWS = BASE + 4 * R
TAIL = 16
NZ = 8
NB = 2 * NZ
NSIDE = 4
SHIFTS = (0, 1, 3, 2)
SPAN = 1024
M = NB * CTR
VM = pl.BlockSpec(memory_space=pltpu.VMEM)
SM = pl.BlockSpec(memory_space=pltpu.SMEM)
PARAMS = pltpu.CompilerParams(vmem_limit_bytes=44 * 2**20)


def dot_nn(a, b):
    return lax.dot_general(a, b, (((1,), (0,)), ((), ())), preferred_element_type=F32)


def fold(v):
    return jnp.sum(v.reshape(v.shape[0] // 8, 8, v.shape[1]), axis=0)


def prep_kernel(x_ref, v_ref, c_ref, s_ref, l_ref, r_ref, ls_ref, pp_ref, cb_ref, lv_ref):
    ls = ls_ref[...]
    x = (x_ref[...].astype(F32) / ls).astype(BF)
    c = (c_ref[...].astype(F32) / ls).astype(BF)
    lt, rt = l_ref[...], r_ref[...]
    pp_ref[...] = jnp.concatenate([x, c, v_ref[:, 0:CTR], v_ref[:, CTR:PTS], rt, lt], 0)
    cb_ref[...] = jnp.concatenate([c, s_ref[...], lt, rt], 0)
    lv_ref[...] = jnp.broadcast_to(ls, lv_ref.shape)


def set_centers(held, ct, hc, ut):
    for j in range(NB):
        h, i = divmod(j, NZ)
        ref, i = (held[2 * h], i) if i < 2 else (held[2 * h + 1], i - 2)
        cols = slice(j * CTR, (j + 1) * CTR)
        t = ref[i, 0:CTR, :].astype(F32).T
        ct[:, cols] = t.astype(BF)
        hc[:, cols] = jnp.broadcast_to(0.5 * jnp.sum(t * t, axis=0, keepdims=True), (8, CTR))
        ut[0 : 3 * R, cols] = ref[i, CTR:CROWS, :]
        ut[3 * R : D, cols] = jnp.zeros((R, CTR), BF)


def turn(rows, vrows, first, xt, hx, vs, slot, at):
    span = slice(at * 128, (at + 1) * 128)
    f = rows.astype(F32)
    xt[slot, :, span] = f.T.astype(BF)
    hx[slot, span, :] = jnp.broadcast_to(0.5 * jnp.sum(f * f, axis=1, keepdims=True), (128, 128))
    above = [jnp.zeros((first, 128), F32)] if first else []
    below = jnp.zeros((128 - first - vrows.shape[0], 128), F32)
    vs[slot, span, :] = jnp.concatenate(above + [vrows.astype(F32), below], 0).T.astype(BF)


def sweep(x, xt, hx, vs, ct, hc, ut, gt, qt, want_rows):
    n = x.shape[0]
    rows = None
    for m in range(0, M, SPAN):
        cols = slice(m, m + SPAN)
        cross = dot_nn(x, ct[:, cols])
        prod = dot_nn(vs, ut[:, cols])
        parts = []
        for k in range(SPAN // 128):
            part = slice(k * 128, (k + 1) * 128)
            h = hc[0:1, m + k * 128 : m + (k + 1) * 128]
            parts.append(jnp.exp((cross[:, part] - hx) - h) * prod[:, part])
        w = jnp.concatenate(parts, 1)
        gt[:, cols] += dot_nn(xt, w.astype(BF))
        qt[:, cols] += fold(w)
        if want_rows:
            for p in parts:
                rows = p if rows is None else rows + p
    return rows


def add_pairs(blocks, count, ct, hc, ut, gt, qt, xt, hx, vs, yt, hy, us):
    gt[...] = jnp.zeros_like(gt)
    qt[...] = jnp.zeros_like(qt)
    steps = count // NSIDE

    def turn_points(a, slot):
        for k in range(2 * NSIDE):
            i, h = NSIDE * a + k // 2, k % 2
            vrows = blocks[i, BASE + h * R : BASE + (h + 1) * R, :]
            turn(blocks[i, h * 128 : (h + 1) * 128, :], vrows, 0, xt, hx, vs, slot, k)

    def turn_centers(a):
        for k in range(NSIDE):
            i = NSIDE * a + k
            turn(blocks[i, PTS:BASE, :], blocks[i, BASE + 2 * R : PROWS, :], R, yt, hy, us, a, k)

    def points_step(a, ell):
        slot = lax.rem(a, 2)
        x = jnp.concatenate([blocks[NSIDE * a + k, 0:PTS, :] for k in range(NSIDE)], 0)
        rows = sweep(x, xt[slot], hx[slot], vs[slot], ct, hc, ut, gt, qt, True)
        if steps > 1:
            turn_points(lax.min(a + 1, steps - 1), 1 - slot)
        turn_centers(a)
        xf = x.astype(F32)
        return ell + fold(jnp.sum(rows, axis=1, keepdims=True) * (xf * xf))

    turn_points(0, 0)
    ell = lax.fori_loop(0, steps, points_step, jnp.zeros((8, D), F32))
    both = jnp.zeros((D, CTR), F32)
    for j in range(NB):
        cols = slice(j * CTR, (j + 1) * CTR)
        both = both + ct[:, cols].astype(F32) * gt[:, cols]
    c = jnp.concatenate([blocks[i, PTS:BASE, :] for i in range(count)], 0)
    yts, hys, uss = (
        jnp.concatenate([ref[a] for a in range(steps)], axis) for ref, axis in ((yt, 1), (hy, 0), (us, 0))
    )
    sweep(c, yts, hys, uss, ct, hc, ut, gt, qt, False)
    return ell, both


def block_terms(j, ct, gt, qt):
    cols = slice(j * CTR, (j + 1) * CTR)
    c = ct[:, cols].astype(F32)
    q = jnp.sum(qt[:, cols], axis=0, keepdims=True)
    t = gt[:, cols] - q * c
    return t, c * t


def first_kernel(h0, h1, h2, h3, a_ref, b_ref, c_ref, d_ref, lv_ref, ct, hc, ut, t_ref, s_ref, gt, qt, *work):
    set_centers((h0, h1, h2, h3), ct, hc, ut)
    blocks = work[-1]
    for k, ref in enumerate((a_ref, b_ref, c_ref, d_ref)):
        blocks[k] = ref[...]
    ell, both = add_pairs(blocks, NSIDE, ct, hc, ut, gt, qt, *work[:-1])
    for j in range(NB):
        t, s = block_terms(j, ct, gt, qt)
        t_ref[:, j * CTR : (j + 1) * CTR] = t
        both = both + s
    s_ref[0:8, :] = ell - fold(both.T)
    s_ref[8:16, :] = lv_ref[...]


def middle_kernel(ct, hc, ut, t0, s0, a_ref, b_ref, t_ref, s_ref, gt, qt, *work):
    blocks = work[-1]
    for k, ref in enumerate((a_ref, b_ref)):
        for i in range(NSIDE):
            blocks[NSIDE * k + i] = ref[i]
    ell, both = add_pairs(blocks, 2 * NSIDE, ct, hc, ut, gt, qt, *work[:-1])
    for j in range(NB):
        cols = slice(j * CTR, (j + 1) * CTR)
        t, s = block_terms(j, ct, gt, qt)
        t_ref[:, cols] = t0[:, cols] + t
        both = both + s
    s_ref[0:8, :] = s0[0:8, :] + ell - fold(both.T)
    s_ref[8:16, :] = s0[8:16, :]


def last_kernel(at_ref, ct, hc, ut, t0, s0, a_ref, t_ref, s_ref, gt, qt, *work):
    blocks = work[-1]
    for i in range(NSIDE):
        blocks[i] = a_ref[i]
    ell, both = add_pairs(blocks, NSIDE, ct, hc, ut, gt, qt, *work[:-1])
    inv = 1.0 / s0[8:9, :]
    zh = at_ref[0]
    for j in range(NB):
        t, s = block_terms(j, ct, gt, qt)
        both = both + s
        h, i = divmod(j, NZ)
        t_ref[h, i % 2, lax.rem(zh + 4 - SHIFTS[i // 2], 4)] = (t0[:, j * CTR : (j + 1) * CTR] + t).T * inv
    scale = jnp.sum(s0[0:8, :] + ell - fold(both.T), axis=0, keepdims=True)
    s_ref[...] = jnp.broadcast_to(scale[None], s_ref.shape)


def shifted(value, axis, by):
    n = dict(zip(AXES, SIZES))[axis]
    return lax.ppermute(value, axis, [(i, (i + by) % n) for i in range(n)])


def plane_shift(value, by, swap):
    perm = []
    for y in range(4):
        for core in range(2):
            for x in range(4):
                along_x = (core == 0) != swap
                ty, tx = (y, (x + by) % 4) if along_x else ((y + by) % 4, x)
                perm.append(((y * 2 + core) * 4 + x, (ty * 2 + core) * 4 + tx))
    return lax.ppermute(value, PLANE_AXES, perm)


def pieces(s):
    a = s.astype(BF)
    rest = s - a.astype(F32)
    b = rest.astype(BF)
    c = (rest - b.astype(F32)).astype(BF)
    return jnp.concatenate([jnp.stack([a, b, c]), jnp.zeros((TAIL - 3, D), BF)], 0)


def cost(peers):
    rows = peers * BASE
    return pl.CostEstimate(flops=2 * rows * M * 288, bytes_accessed=2**22, transcendentals=rows * M)


def work_space(count):
    n, nc, steps = NSIDE * PTS, NSIDE * CTR, count // NSIDE
    return [
        pltpu.VMEM((D, M), F32),
        pltpu.VMEM((8, M), F32),
        pltpu.VMEM((2, D, n), BF),
        pltpu.VMEM((2, n, 128), F32),
        pltpu.VMEM((2, n, 128), BF),
        pltpu.VMEM((steps, D, nc), BF),
        pltpu.VMEM((steps, nc, 128), F32),
        pltpu.VMEM((steps, nc, 128), BF),
        pltpu.VMEM((count, PROWS, D), BF),
    ]


def first_call(*args):
    shape = jax.ShapeDtypeStruct
    return pl.pallas_call(
        first_kernel,
        out_shape=[
            shape((D, M), BF),
            shape((8, M), F32),
            shape((D, M), BF),
            shape((D, M), F32),
            shape((16, D), F32),
        ],
        in_specs=[VM] * 9,
        out_specs=[VM] * 5,
        scratch_shapes=work_space(NSIDE),
        compiler_params=PARAMS,
        cost_estimate=pl.CostEstimate(flops=1, bytes_accessed=1, transcendentals=0),
        name="pairs_first",
    )(*args)


def middle_call(*args):
    shape = jax.ShapeDtypeStruct
    return pl.pallas_call(
        middle_kernel,
        out_shape=[shape((D, M), F32), shape((16, D), F32)],
        in_specs=[VM] * 7,
        out_specs=[VM] * 2,
        scratch_shapes=work_space(2 * NSIDE),
        compiler_params=PARAMS,
        cost_estimate=pl.CostEstimate(flops=1, bytes_accessed=1, transcendentals=0),
        name="pairs_middle",
    )(*args)


def last_call(*args):
    shape = jax.ShapeDtypeStruct
    return pl.pallas_call(
        last_kernel,
        out_shape=[shape((2, 2, NZ // 2, CTR, D), F32), shape((64, 1, D), F32)],
        in_specs=[SM] + [VM] * 6,
        out_specs=[VM] * 2,
        scratch_shapes=work_space(NSIDE),
        compiler_params=PARAMS,
        cost_estimate=cost(NSIDE),
        name="pairs_last",
    )(*args)


def local(points, adjoint_rows, centers, solution_rows, center_left, center_right, lengthscale):
    ls = lengthscale.reshape(1, D)
    shape = jax.ShapeDtypeStruct
    pp, cb, lv = pl.pallas_call(
        prep_kernel,
        out_shape=[shape((PROWS, D), BF), shape((CROWS, D), BF), shape((8, D), F32)],
        in_specs=[VM] * 7,
        out_specs=[VM] * 3,
        name="prep",
    )(points, adjoint_rows.T, centers, solution_rows.T, center_left.T, center_right.T, ls)
    side = [pp] + [plane_shift(pp, by, False) for by in (1, 3, 2)]
    two = jnp.stack([cb, shifted(cb, "zl", 1)])
    line = jnp.stack(side)
    rest = [plane_shift(line, by, True) for by in (1, 3, 2)]
    two_other = shifted(two, "core", 1)
    six = jnp.concatenate([shifted(two, "zh", by) for by in SHIFTS[1:]], 0)
    held = (two, six, two_other, shifted(six, "core", 1))
    at = lax.axis_index("zh").astype(jnp.int32).reshape(1)
    state = list(first_call(*held, *side, lv))
    state[3:5] = middle_call(*state, *rest[1:])
    terms, scale = last_call(at, *state, rest[0])
    half = terms[0, 0] + shifted(terms[1, 0], "core", 1)
    half = half + shifted(terms[0, 1].astype(BF), "zl", 1).astype(F32)
    cross = [(2 * a + b, 2 * (1 - a) + 1 - b) for a in range(2) for b in range(2)]
    half = half + lax.ppermute(terms[1, 1].astype(BF), ("core", "zl"), cross).astype(F32)
    scale = jnp.sum(lax.all_to_all(scale, SCALE_AXES, 0, 0, tiled=True), (0, 1))
    tail = jnp.broadcast_to(pieces(scale)[None], (NZ // 2, TAIL, D))
    parts = lax.all_to_all(jnp.concatenate([half.astype(BF), tail], 1), "zh", 0, 0, tiled=True)
    total = jnp.sum(parts[:, 0:CTR].astype(F32), 0)
    return total, jnp.sum(parts[:, CTR:].astype(F32), (0, 1)) / lv[0]


def solution(mesh):
    grid = Mesh(mesh.devices.reshape(SIZES), AXES)
    rows = P(AXES, None)
    return jax.shard_map(
        local,
        mesh=grid,
        in_specs=(rows,) * 6 + (P(),),
        out_specs=(rows, P()),
        check_vma=False,
    )
```

```python
import functools

import jax
import jax.numpy as jnp
from jax import lax
from jax.experimental import pallas as pl
from jax.experimental.pallas import tpu as pltpu
from jax.sharding import Mesh, PartitionSpec as P

BF = jnp.bfloat16
F32 = jnp.float32
AXES = ("zh", "y", "core", "zl", "x")
SIZES = (4, 4, 2, 2, 4)
CENTER_AXES = ("zh", "zl")
PLANE_AXES = ("y", "core", "x")
SCALE_AXES = ("y", "x", "core")
D = 128
R = 32
PTS = 256
CTR = 128
CROWS = CTR + 3 * R
BASE = PTS + CTR
PROWS = BASE + 4 * R
TAIL = 16
NZ = 8
NB = 2 * NZ
NSIDE = 4
SHIFTS = (0, 1, 3, 2)
SPAN = 1024
M = NB * CTR
VM = pl.BlockSpec(memory_space=pltpu.VMEM)
SM = pl.BlockSpec(memory_space=pltpu.SMEM)
PARAMS = pltpu.CompilerParams(vmem_limit_bytes=44 * 2**20)


def dot_nn(a, b):
    return lax.dot_general(a, b, (((1,), (0,)), ((), ())), preferred_element_type=F32)


def fold(v):
    return jnp.sum(v.reshape(v.shape[0] // 8, 8, v.shape[1]), axis=0)


def prep_kernel(x_ref, v_ref, c_ref, s_ref, l_ref, r_ref, ls_ref, pp_ref, cb_ref, lv_ref):
    ls = ls_ref[...]
    x = (x_ref[...].astype(F32) / ls).astype(BF)
    c = (c_ref[...].astype(F32) / ls).astype(BF)
    lt, rt = l_ref[...], r_ref[...]
    pp_ref[...] = jnp.concatenate([x, c, v_ref[:, 0:CTR], v_ref[:, CTR:PTS], rt, lt], 0)
    cb_ref[...] = jnp.concatenate([c, s_ref[...], lt, rt], 0)
    lv_ref[...] = jnp.broadcast_to(ls, lv_ref.shape)


def set_centers(held, ct, hc, ut):
    for j in range(NB):
        h, i = divmod(j, NZ)
        ref, i = (held[2 * h], i) if i < 2 else (held[2 * h + 1], i - 2)
        cols = slice(j * CTR, (j + 1) * CTR)
        t = ref[i, 0:CTR, :].astype(F32).T
        ct[:, cols] = t.astype(BF)
        hc[:, cols] = jnp.broadcast_to(0.5 * jnp.sum(t * t, axis=0, keepdims=True), (8, CTR))
        ut[0 : 3 * R, cols] = ref[i, CTR:CROWS, :]
        ut[3 * R : D, cols] = jnp.zeros((R, CTR), BF)


def turn(rows, vrows, first, xt, hx, vs, slot, at):
    span = slice(at * 128, (at + 1) * 128)
    f = rows.astype(F32)
    xt[slot, :, span] = f.T.astype(BF)
    hx[slot, span, :] = jnp.broadcast_to(0.5 * jnp.sum(f * f, axis=1, keepdims=True), (128, 128))
    above = [jnp.zeros((first, 128), F32)] if first else []
    below = jnp.zeros((128 - first - vrows.shape[0], 128), F32)
    vs[slot, span, :] = jnp.concatenate(above + [vrows.astype(F32), below], 0).T.astype(BF)


def sweep(x, xt, hx, vs, ct, hc, ut, gt, qt, want_rows):
    n = x.shape[0]
    rows = None
    for m in range(0, M, SPAN):
        cols = slice(m, m + SPAN)
        cross = dot_nn(x, ct[:, cols])
        prod = dot_nn(vs, ut[:, cols])
        parts = []
        for k in range(SPAN // 128):
            part = slice(k * 128, (k + 1) * 128)
            h = hc[0:1, m + k * 128 : m + (k + 1) * 128]
            parts.append(jnp.exp((cross[:, part] - hx) - h) * prod[:, part])
        w = jnp.concatenate(parts, 1)
        gt[:, cols] += dot_nn(xt, w.astype(BF))
        qt[:, cols] += fold(w)
        if want_rows:
            for p in parts:
                rows = p if rows is None else rows + p
    return rows


def add_pairs(blocks, count, ct, hc, ut, gt, qt, xt, hx, vs, yt, hy, us):
    gt[...] = jnp.zeros_like(gt)
    qt[...] = jnp.zeros_like(qt)
    steps = count // NSIDE

    def turn_points(a, slot):
        for k in range(2 * NSIDE):
            i, h = NSIDE * a + k // 2, k % 2
            vrows = blocks[i, BASE + h * R : BASE + (h + 1) * R, :]
            turn(blocks[i, h * 128 : (h + 1) * 128, :], vrows, 0, xt, hx, vs, slot, k)

    def turn_centers(a):
        for k in range(NSIDE):
            i = NSIDE * a + k
            turn(blocks[i, PTS:BASE, :], blocks[i, BASE + 2 * R : PROWS, :], R, yt, hy, us, a, k)

    def points_step(a, ell):
        slot = lax.rem(a, 2)
        x = jnp.concatenate([blocks[NSIDE * a + k, 0:PTS, :] for k in range(NSIDE)], 0)
        rows = sweep(x, xt[slot], hx[slot], vs[slot], ct, hc, ut, gt, qt, True)
        if steps > 1:
            turn_points(lax.min(a + 1, steps - 1), 1 - slot)
        turn_centers(a)
        xf = x.astype(F32)
        return ell + fold(jnp.sum(rows, axis=1, keepdims=True) * (xf * xf))

    turn_points(0, 0)
    ell = lax.fori_loop(0, steps, points_step, jnp.zeros((8, D), F32))
    both = jnp.zeros((D, CTR), F32)
    for j in range(NB):
        cols = slice(j * CTR, (j + 1) * CTR)
        both = both + ct[:, cols].astype(F32) * gt[:, cols]
    c = jnp.concatenate([blocks[i, PTS:BASE, :] for i in range(count)], 0)
    yts, hys, uss = (
        jnp.concatenate([ref[a] for a in range(steps)], axis) for ref, axis in ((yt, 1), (hy, 0), (us, 0))
    )
    sweep(c, yts, hys, uss, ct, hc, ut, gt, qt, False)
    return ell, both


def block_terms(j, ct, gt, qt):
    cols = slice(j * CTR, (j + 1) * CTR)
    c = ct[:, cols].astype(F32)
    q = jnp.sum(qt[:, cols], axis=0, keepdims=True)
    t = gt[:, cols] - q * c
    return t, c * t


def first_kernel(h0, h1, h2, h3, a_ref, b_ref, c_ref, d_ref, lv_ref, ct, hc, ut, t_ref, s_ref, gt, qt, *work):
    set_centers((h0, h1, h2, h3), ct, hc, ut)
    blocks = work[-1]
    for k, ref in enumerate((a_ref, b_ref, c_ref, d_ref)):
        blocks[k] = ref[...]
    ell, both = add_pairs(blocks, NSIDE, ct, hc, ut, gt, qt, *work[:-1])
    for j in range(NB):
        t, s = block_terms(j, ct, gt, qt)
        t_ref[:, j * CTR : (j + 1) * CTR] = t
        both = both + s
    s_ref[0:8, :] = ell - fold(both.T)
    s_ref[8:16, :] = lv_ref[...]


def middle_kernel(ct, hc, ut, t0, s0, a_ref, b_ref, t_ref, s_ref, gt, qt, *work):
    blocks = work[-1]
    for k, ref in enumerate((a_ref, b_ref)):
        for i in range(NSIDE):
            blocks[NSIDE * k + i] = ref[i]
    ell, both = add_pairs(blocks, 2 * NSIDE, ct, hc, ut, gt, qt, *work[:-1])
    for j in range(NB):
        cols = slice(j * CTR, (j + 1) * CTR)
        t, s = block_terms(j, ct, gt, qt)
        t_ref[:, cols] = t0[:, cols] + t
        both = both + s
    s_ref[0:8, :] = s0[0:8, :] + ell - fold(both.T)
    s_ref[8:16, :] = s0[8:16, :]


def last_kernel(at_ref, ct, hc, ut, t0, s0, a_ref, t_ref, s_ref, gt, qt, *work):
    blocks = work[-1]
    for i in range(NSIDE):
        blocks[i] = a_ref[i]
    ell, both = add_pairs(blocks, NSIDE, ct, hc, ut, gt, qt, *work[:-1])
    inv = 1.0 / s0[8:9, :]
    zh, zl = at_ref[0], at_ref[1]
    for j in range(NB):
        t, s = block_terms(j, ct, gt, qt)
        both = both + s
        h, i = divmod(j, NZ)
        place = lax.rem(zh + 4 - SHIFTS[i // 2], 4) * 2 + (zl if i % 2 == 0 else 1 - zl)
        t_ref[h, place] = (t0[:, j * CTR : (j + 1) * CTR] + t).T * inv
    scale = jnp.sum(s0[0:8, :] + ell - fold(both.T), axis=0, keepdims=True)
    s_ref[...] = jnp.broadcast_to(scale[None], s_ref.shape)


def shifted(value, axis, by):
    n = dict(zip(AXES, SIZES))[axis]
    return lax.ppermute(value, axis, [(i, (i + by) % n) for i in range(n)])


def plane_shift(value, by, swap):
    perm = []
    for y in range(4):
        for core in range(2):
            for x in range(4):
                along_x = (core == 0) != swap
                ty, tx = (y, (x + by) % 4) if along_x else ((y + by) % 4, x)
                perm.append(((y * 2 + core) * 4 + x, (ty * 2 + core) * 4 + tx))
    return lax.ppermute(value, PLANE_AXES, perm)


def pieces(s):
    a = s.astype(BF)
    rest = s - a.astype(F32)
    b = rest.astype(BF)
    c = (rest - b.astype(F32)).astype(BF)
    return jnp.concatenate([jnp.stack([a, b, c]), jnp.zeros((TAIL - 3, D), BF)], 0)


def cost(peers):
    rows = peers * BASE
    return pl.CostEstimate(flops=2 * rows * M * 288, bytes_accessed=2**22, transcendentals=rows * M)


def work_space(count):
    n, nc, steps = NSIDE * PTS, NSIDE * CTR, count // NSIDE
    return [
        pltpu.VMEM((D, M), F32),
        pltpu.VMEM((8, M), F32),
        pltpu.VMEM((2, D, n), BF),
        pltpu.VMEM((2, n, 128), F32),
        pltpu.VMEM((2, n, 128), BF),
        pltpu.VMEM((steps, D, nc), BF),
        pltpu.VMEM((steps, nc, 128), F32),
        pltpu.VMEM((steps, nc, 128), BF),
        pltpu.VMEM((count, PROWS, D), BF),
    ]


def first_call(*args):
    shape = jax.ShapeDtypeStruct
    return pl.pallas_call(
        first_kernel,
        out_shape=[
            shape((D, M), BF),
            shape((8, M), F32),
            shape((D, M), BF),
            shape((D, M), F32),
            shape((16, D), F32),
        ],
        in_specs=[VM] * 9,
        out_specs=[VM] * 5,
        scratch_shapes=work_space(NSIDE),
        compiler_params=PARAMS,
        cost_estimate=pl.CostEstimate(flops=1, bytes_accessed=1, transcendentals=0),
        name="pairs_first",
    )(*args)


def middle_call(*args):
    shape = jax.ShapeDtypeStruct
    return pl.pallas_call(
        middle_kernel,
        out_shape=[shape((D, M), F32), shape((16, D), F32)],
        in_specs=[VM] * 7,
        out_specs=[VM] * 2,
        scratch_shapes=work_space(2 * NSIDE),
        compiler_params=PARAMS,
        cost_estimate=pl.CostEstimate(flops=1, bytes_accessed=1, transcendentals=0),
        name="pairs_middle",
    )(*args)


def last_call(*args):
    shape = jax.ShapeDtypeStruct
    return pl.pallas_call(
        last_kernel,
        out_shape=[shape((2, NZ, CTR, D), F32), shape((32, 1, D), F32)],
        in_specs=[SM] + [VM] * 6,
        out_specs=[VM] * 2,
        scratch_shapes=work_space(NSIDE),
        compiler_params=PARAMS,
        cost_estimate=cost(NSIDE),
        name="pairs_last",
    )(*args)


def local(points, adjoint_rows, centers, solution_rows, center_left, center_right, lengthscale):
    ls = lengthscale.reshape(1, D)
    shape = jax.ShapeDtypeStruct
    pp, cb, lv = pl.pallas_call(
        prep_kernel,
        out_shape=[shape((PROWS, D), BF), shape((CROWS, D), BF), shape((8, D), F32)],
        in_specs=[VM] * 7,
        out_specs=[VM] * 3,
        name="prep",
    )(points, adjoint_rows.T, centers, solution_rows.T, center_left.T, center_right.T, ls)
    side = [pp] + [plane_shift(pp, by, False) for by in (1, 3, 2)]
    two = jnp.stack([cb, shifted(cb, "zl", 1)])
    line = jnp.stack(side)
    rest = [plane_shift(line, by, True) for by in (2, 1, 3)]
    two_other = shifted(two, "core", 1)
    six = jnp.concatenate([shifted(two, "zh", by) for by in SHIFTS[1:]], 0)
    held = (two, six, two_other, shifted(six, "core", 1))
    at = jnp.stack([lax.axis_index("zh"), lax.axis_index("zl")]).astype(jnp.int32)
    state = list(first_call(*held, *side, lv))
    state[3:5] = middle_call(*state, *rest[1:])
    terms, scale = last_call(at, *state, rest[0])
    swapped = shifted(terms[1], "core", 1)
    scale = jnp.sum(lax.all_to_all(scale, SCALE_AXES, 0, 0, tiled=True), (0, 1))
    mine = (terms[0] + swapped).astype(BF)
    chunk = jnp.concatenate([mine, jnp.broadcast_to(pieces(scale)[None], (NZ, TAIL, D))], 1)
    parts = lax.all_to_all(chunk, CENTER_AXES, 0, 0, tiled=True)
    total = jnp.sum(parts[:, 0:CTR].astype(F32), 0)
    return total, jnp.sum(parts[:, CTR:].astype(F32), (0, 1)) / lv[0]


def solution(mesh):
    grid = Mesh(mesh.devices.reshape(SIZES), AXES)
    rows = P(AXES, None)
    return jax.shard_map(
        local,
        mesh=grid,
        in_specs=(rows,) * 6 + (P(),),
        out_specs=(rows, P()),
        check_vma=False,
    )
```

```python
import functools

import jax
import jax.numpy as jnp
from jax import lax
from jax.experimental import pallas as pl
from jax.experimental.pallas import tpu as pltpu
from jax.sharding import Mesh, PartitionSpec as P

BF = jnp.bfloat16
F32 = jnp.float32
AXES = ("zh", "y", "core", "zl", "x")
SIZES = (4, 4, 2, 2, 4)
CENTER_AXES = ("zh", "zl")
PLANE_AXES = ("y", "core", "x")
SCALE_AXES = ("y", "x", "core")
D = 128
R = 32
PTS = 256
CTR = 128
CROWS = CTR + 3 * R
BASE = PTS + CTR
PROWS = BASE + 4 * R
TAIL = 16
NZ = 8
NB = 2 * NZ
NSIDE = 4
SHIFTS = (0, 1, 3, 2)
SPAN = 1024
M = NB * CTR
VM = pl.BlockSpec(memory_space=pltpu.VMEM)
SM = pl.BlockSpec(memory_space=pltpu.SMEM)
PARAMS = pltpu.CompilerParams(vmem_limit_bytes=44 * 2**20)


def dot_nn(a, b):
    return lax.dot_general(a, b, (((1,), (0,)), ((), ())), preferred_element_type=F32)


def fold(v):
    return jnp.sum(v.reshape(v.shape[0] // 8, 8, v.shape[1]), axis=0)


def prep_kernel(x_ref, v_ref, c_ref, s_ref, l_ref, r_ref, ls_ref, pp_ref, cb_ref, lv_ref):
    ls = ls_ref[...]
    x = (x_ref[...].astype(F32) / ls).astype(BF)
    c = (c_ref[...].astype(F32) / ls).astype(BF)
    lt, rt = l_ref[...], r_ref[...]
    pp_ref[...] = jnp.concatenate([x, c, v_ref[:, 0:CTR], v_ref[:, CTR:PTS], rt, lt], 0)
    cb_ref[0] = jnp.concatenate([c, s_ref[...], lt, rt], 0)
    cb_ref[1] = jnp.zeros((CROWS, D), BF)
    lv_ref[...] = jnp.broadcast_to(ls, lv_ref.shape)


def set_centers(held, ct, hc, ut):
    for j in range(NB):
        h, i = divmod(j, NZ)
        ref, i = (held[2 * h], i) if i < 2 else (held[2 * h + 1], i - 2)
        cols = slice(j * CTR, (j + 1) * CTR)
        t = ref[i, 0:CTR, :].astype(F32).T
        ct[:, cols] = t.astype(BF)
        hc[:, cols] = jnp.broadcast_to(0.5 * jnp.sum(t * t, axis=0, keepdims=True), (8, CTR))
        ut[0 : 3 * R, cols] = ref[i, CTR:CROWS, :]
        ut[3 * R : D, cols] = jnp.zeros((R, CTR), BF)


def turn(rows, vrows, first, xt, hx, vs, slot, at):
    span = slice(at * 128, (at + 1) * 128)
    f = rows.astype(F32)
    xt[slot, :, span] = f.T.astype(BF)
    hx[slot, span, :] = jnp.broadcast_to(0.5 * jnp.sum(f * f, axis=1, keepdims=True), (128, 128))
    above = [jnp.zeros((first, 128), F32)] if first else []
    below = jnp.zeros((128 - first - vrows.shape[0], 128), F32)
    vs[slot, span, :] = jnp.concatenate(above + [vrows.astype(F32), below], 0).T.astype(BF)


def sweep(x, xt, hx, vs, ct, hc, ut, gt, qt, want_rows):
    n = x.shape[0]
    rows = None
    for m in range(0, M, SPAN):
        cols = slice(m, m + SPAN)
        cross = dot_nn(x, ct[:, cols])
        prod = dot_nn(vs, ut[:, cols])
        parts = []
        for k in range(SPAN // 128):
            part = slice(k * 128, (k + 1) * 128)
            h = hc[0:1, m + k * 128 : m + (k + 1) * 128]
            parts.append(jnp.exp((cross[:, part] - hx) - h) * prod[:, part])
        w = jnp.concatenate(parts, 1)
        gt[:, cols] += dot_nn(xt, w.astype(BF))
        qt[:, cols] += fold(w)
        if want_rows:
            for p in parts:
                rows = p if rows is None else rows + p
    return rows


def add_pairs(blocks, count, ct, hc, ut, gt, qt, xt, hx, vs, yt, hy, us):
    gt[...] = jnp.zeros_like(gt)
    qt[...] = jnp.zeros_like(qt)
    steps = count // NSIDE

    def turn_points(a, slot):
        for k in range(2 * NSIDE):
            i, h = NSIDE * a + k // 2, k % 2
            vrows = blocks[i, BASE + h * R : BASE + (h + 1) * R, :]
            turn(blocks[i, h * 128 : (h + 1) * 128, :], vrows, 0, xt, hx, vs, slot, k)

    def turn_centers(a):
        for k in range(NSIDE):
            i = NSIDE * a + k
            turn(blocks[i, PTS:BASE, :], blocks[i, BASE + 2 * R : PROWS, :], R, yt, hy, us, a, k)

    def points_step(a, ell):
        slot = lax.rem(a, 2)
        x = jnp.concatenate([blocks[NSIDE * a + k, 0:PTS, :] for k in range(NSIDE)], 0)
        rows = sweep(x, xt[slot], hx[slot], vs[slot], ct, hc, ut, gt, qt, True)
        if steps > 1:
            turn_points(lax.min(a + 1, steps - 1), 1 - slot)
        turn_centers(a)
        xf = x.astype(F32)
        return ell + fold(jnp.sum(rows, axis=1, keepdims=True) * (xf * xf))

    turn_points(0, 0)
    ell = lax.fori_loop(0, steps, points_step, jnp.zeros((8, D), F32))
    both = jnp.zeros((D, CTR), F32)
    for j in range(NB):
        cols = slice(j * CTR, (j + 1) * CTR)
        both = both + ct[:, cols].astype(F32) * gt[:, cols]
    c = jnp.concatenate([blocks[i, PTS:BASE, :] for i in range(count)], 0)
    yts, hys, uss = (
        jnp.concatenate([ref[a] for a in range(steps)], axis) for ref, axis in ((yt, 1), (hy, 0), (us, 0))
    )
    sweep(c, yts, hys, uss, ct, hc, ut, gt, qt, False)
    return ell, both


def block_terms(j, ct, gt, qt):
    cols = slice(j * CTR, (j + 1) * CTR)
    c = ct[:, cols].astype(F32)
    q = jnp.sum(qt[:, cols], axis=0, keepdims=True)
    t = gt[:, cols] - q * c
    return t, c * t


def first_kernel(h0, h1, h2, h3, a_ref, b_ref, c_ref, d_ref, lv_ref, ct, hc, ut, t_ref, s_ref, gt, qt, *work):
    set_centers((h0, h1, h2, h3), ct, hc, ut)
    blocks = work[-1]
    for k, ref in enumerate((a_ref, b_ref, c_ref, d_ref)):
        blocks[k] = ref[...]
    ell, both = add_pairs(blocks, NSIDE, ct, hc, ut, gt, qt, *work[:-1])
    for j in range(NB):
        t, s = block_terms(j, ct, gt, qt)
        t_ref[:, j * CTR : (j + 1) * CTR] = t
        both = both + s
    s_ref[0:8, :] = ell - fold(both.T)
    s_ref[8:16, :] = lv_ref[...]


def middle_kernel(ct, hc, ut, t0, s0, a_ref, b_ref, t_ref, s_ref, gt, qt, *work):
    blocks = work[-1]
    for k, ref in enumerate((a_ref, b_ref)):
        for i in range(NSIDE):
            blocks[NSIDE * k + i] = ref[i]
    ell, both = add_pairs(blocks, 2 * NSIDE, ct, hc, ut, gt, qt, *work[:-1])
    for j in range(NB):
        cols = slice(j * CTR, (j + 1) * CTR)
        t, s = block_terms(j, ct, gt, qt)
        t_ref[:, cols] = t0[:, cols] + t
        both = both + s
    s_ref[0:8, :] = s0[0:8, :] + ell - fold(both.T)
    s_ref[8:16, :] = s0[8:16, :]


def last_kernel(at_ref, ct, hc, ut, t0, s0, a_ref, t_ref, s_ref, gt, qt, *work):
    blocks = work[-1]
    for i in range(NSIDE):
        blocks[i] = a_ref[i]
    ell, both = add_pairs(blocks, NSIDE, ct, hc, ut, gt, qt, *work[:-1])
    inv = 1.0 / s0[8:9, :]
    zh, zl = at_ref[0], at_ref[1]
    for j in range(NB):
        t, s = block_terms(j, ct, gt, qt)
        both = both + s
        h, i = divmod(j, NZ)
        place = lax.rem(zh + 4 - SHIFTS[i // 2], 4) * 2 + (zl if i % 2 == 0 else 1 - zl)
        t_ref[h, place] = (t0[:, j * CTR : (j + 1) * CTR] + t).T * inv
    scale = jnp.sum(s0[0:8, :] + ell - fold(both.T), axis=0, keepdims=True)
    s_ref[...] = jnp.broadcast_to(scale[None], s_ref.shape)


def shifted(value, axis, by):
    n = dict(zip(AXES, SIZES))[axis]
    return lax.ppermute(value, axis, [(i, (i + by) % n) for i in range(n)])


def plane_shift(value, by, swap):
    perm = []
    for y in range(4):
        for core in range(2):
            for x in range(4):
                along_x = (core == 0) != swap
                ty, tx = (y, (x + by) % 4) if along_x else ((y + by) % 4, x)
                perm.append(((y * 2 + core) * 4 + x, (ty * 2 + core) * 4 + tx))
    return lax.ppermute(value, PLANE_AXES, perm)


def pieces(s):
    a = s.astype(BF)
    rest = s - a.astype(F32)
    b = rest.astype(BF)
    c = (rest - b.astype(F32)).astype(BF)
    return jnp.concatenate([jnp.stack([a, b, c]), jnp.zeros((TAIL - 3, D), BF)], 0)


def cost(peers):
    rows = peers * BASE
    return pl.CostEstimate(flops=2 * rows * M * 288, bytes_accessed=2**22, transcendentals=rows * M)


def work_space(count):
    n, nc, steps = NSIDE * PTS, NSIDE * CTR, count // NSIDE
    return [
        pltpu.VMEM((D, M), F32),
        pltpu.VMEM((8, M), F32),
        pltpu.VMEM((2, D, n), BF),
        pltpu.VMEM((2, n, 128), F32),
        pltpu.VMEM((2, n, 128), BF),
        pltpu.VMEM((steps, D, nc), BF),
        pltpu.VMEM((steps, nc, 128), F32),
        pltpu.VMEM((steps, nc, 128), BF),
        pltpu.VMEM((count, PROWS, D), BF),
    ]


def first_call(*args):
    shape = jax.ShapeDtypeStruct
    return pl.pallas_call(
        first_kernel,
        out_shape=[
            shape((D, M), BF),
            shape((8, M), F32),
            shape((D, M), BF),
            shape((D, M), F32),
            shape((16, D), F32),
        ],
        in_specs=[VM] * 9,
        out_specs=[VM] * 5,
        scratch_shapes=work_space(NSIDE),
        compiler_params=PARAMS,
        cost_estimate=pl.CostEstimate(flops=1, bytes_accessed=1, transcendentals=0),
        name="pairs_first",
    )(*args)


def middle_call(*args):
    shape = jax.ShapeDtypeStruct
    return pl.pallas_call(
        middle_kernel,
        out_shape=[shape((D, M), F32), shape((16, D), F32)],
        in_specs=[VM] * 7,
        out_specs=[VM] * 2,
        scratch_shapes=work_space(2 * NSIDE),
        compiler_params=PARAMS,
        cost_estimate=pl.CostEstimate(flops=1, bytes_accessed=1, transcendentals=0),
        name="pairs_middle",
    )(*args)


def last_call(*args):
    shape = jax.ShapeDtypeStruct
    return pl.pallas_call(
        last_kernel,
        out_shape=[shape((2, NZ, CTR, D), F32), shape((32, 1, D), F32)],
        in_specs=[SM] + [VM] * 6,
        out_specs=[VM] * 2,
        scratch_shapes=work_space(NSIDE),
        compiler_params=PARAMS,
        cost_estimate=cost(NSIDE),
        name="pairs_last",
    )(*args)


def local(points, adjoint_rows, centers, solution_rows, center_left, center_right, lengthscale):
    ls = lengthscale.reshape(1, D)
    shape = jax.ShapeDtypeStruct
    pp, cb, lv = pl.pallas_call(
        prep_kernel,
        out_shape=[shape((PROWS, D), BF), shape((2, CROWS, D), BF), shape((8, D), F32)],
        in_specs=[VM] * 7,
        out_specs=[VM] * 3,
        name="prep",
    )(points, adjoint_rows.T, centers, solution_rows.T, center_left.T, center_right.T, ls)
    side = [pp] + [plane_shift(pp, by, False) for by in (1, 3, 2)]
    two = cb.at[1].set(shifted(cb[0], "zl", 1))
    line = jnp.stack(side)
    rest = [plane_shift(line, by, True) for by in (1, 3, 2)]
    two_other = shifted(two, "core", 1)
    six = jnp.concatenate([shifted(two, "zh", by) for by in SHIFTS[1:]], 0)
    held = (two, six, two_other, shifted(six, "core", 1))
    at = jnp.stack([lax.axis_index("zh"), lax.axis_index("zl")]).astype(jnp.int32)
    state = list(first_call(*held, *side, lv))
    state[3:5] = middle_call(*state, *rest[1:])
    terms, scale = last_call(at, *state, rest[0])
    swapped = shifted(terms[1], "core", 1)
    scale = jnp.sum(lax.all_to_all(scale, SCALE_AXES, 0, 0, tiled=True), (0, 1))
    mine = (terms[0] + swapped).astype(BF)
    chunk = jnp.concatenate([mine, jnp.broadcast_to(pieces(scale)[None], (NZ, TAIL, D))], 1)
    parts = lax.all_to_all(chunk, CENTER_AXES, 0, 0, tiled=True)
    total = jnp.sum(parts[:, 0:CTR].astype(F32), 0)
    return total, jnp.sum(parts[:, CTR:].astype(F32), (0, 1)) / lv[0]


def solution(mesh):
    grid = Mesh(mesh.devices.reshape(SIZES), AXES)
    rows = P(AXES, None)
    return jax.shard_map(
        local,
        mesh=grid,
        in_specs=(rows,) * 6 + (P(),),
        out_specs=(rows, P()),
        check_vma=False,
    )
```
